32 devices in a mesh: expert: 8 (over y, x, core), hidden: 4 (over z).
Axes of the slice: x: 2, y: 2, z: 4, core: 2. Of those that a mesh axis runs over, the one named last changes fastest.
Arguments:
- cotangent: bfloat16 [8192, 2048], P(('expert', 'hidden')), may hold values from -6 to 6
- slot_token: int32 [32, 8, 80], P(('expert', 'hidden')), may hold values from -1 to 255, as said below
- slot_gate: float32 [32, 8, 80], P(('expert', 'hidden')), may hold values from 0.1 to 1
- w_down: bfloat16 [8, 4096, 2048], P('expert', 'hidden'), may hold values from -0.09375 to 0.09375
Outputs:
- hidden_grad: bfloat16 [8, 2048, 4096], P('expert', None, 'hidden')
The draws below stay inside these ranges and needn't reach their ends.
Inputs may be any that keep to these rules, and one draw needn't show every extreme that they name: `slot_token`: on each device and for each expert the live slots come first and name distinct local tokens; a device fills at most 80 slots for one expert. For each expert and each index of the hidden axis, the 8 devices with that index name exactly 512 tokens together, so each expert takes exactly 2048 tokens.
All inputs are finite; a program needn't handle non-finite values.
Results may differ from the reference program's by a relative error of at most 0.0049.
Values may be sent and summed in bfloat16 or wider, within the bound.
A program may use at most 128 MiB of HBM per device.

```python
import jax
import jax.numpy as jnp
from jax import lax

D = 2048
F = 4096
TOK_DEV = 256
EXPERTS = 8
SOURCES = 32
TOKENS = 8192
MEAN = 64
SLOT = 80
CAP = 2048
N_EXPERT = 8
N_HIDDEN = 4


def draw_slot_token(key, part):
    groups = N_HIDDEN
    sources = N_EXPERT
    half_count = sources // 2
    spread = MEAN // 4
    key_order = jax.random.fold_in(key, 11)
    key_shift = jax.random.fold_in(key, 12)
    key_token = jax.random.fold_in(key, 13)
    scores = jax.random.randint(key_order, (EXPERTS, groups, sources), 0, 1 << 20) * sources + jnp.arange(sources, dtype=jnp.int32)
    ranking = jnp.argsort(scores, axis=-1).astype(jnp.int32)
    shifts = jax.random.randint(key_shift, (EXPERTS, groups, half_count), -spread, spread + 1)
    shifts = jnp.where(jnp.arange(half_count)[None, None, :] == 0, spread, shifts)
    by_rank = MEAN + jnp.concatenate([shifts, -shifts], axis=-1)
    inverse = jnp.argsort(ranking, axis=-1).astype(jnp.int32)
    per_source = jnp.take_along_axis(by_rank, inverse, axis=-1)
    per_device = jnp.transpose(per_source, (2, 1, 0)).reshape(SOURCES, EXPERTS)
    token_scores = jax.random.randint(key_token, (SOURCES, EXPERTS, TOK_DEV), 0, 1 << 20) * TOK_DEV + jnp.arange(TOK_DEV, dtype=jnp.int32)
    chosen = jnp.argsort(token_scores, axis=-1)[:, :, :SLOT].astype(jnp.int32)
    live_slot = jnp.arange(SLOT, dtype=jnp.int32)[None, None, :] < per_device[:, :, None]
    return jnp.where(live_slot, chosen, -1).astype(jnp.int32)


def block_scale(rng, extent, cuts, least, high):
    def one(axis_at, shards_of):
        steps = jax.random.uniform(jax.random.fold_in(jax.random.fold_in(rng, 6), axis_at), (shards_of,), jnp.float32, least / len(cuts), high / len(cuts))
        return jnp.repeat(jnp.exp(steps), extent[axis_at] // shards_of).reshape((-1,) + (1,) * (len(extent) - axis_at - 1))

    factor_of = one(*cuts[0])
    for cut in cuts[1:]:
        factor_of = factor_of * one(*cut)
    return factor_of


def noise(stream_key, shape, scale, bound, pieces=(), kind=jnp.bfloat16):
    level = block_scale(stream_key, shape, pieces, -0.22, 0.18) if pieces else 1.0
    result = jax.random.normal(stream_key, shape, jnp.float32) * scale * level
    return jnp.minimum(jnp.maximum(result, -bound), bound).astype(kind)


def setup_inputs(seed: int = 0) -> dict:
    arg_keys = jax.random.split(jax.random.key(seed), 5)
    cotangent = noise(arg_keys[0], (TOKENS, D), 1.0, 6.0, ((0, 32),))
    slot_token = draw_slot_token(jax.random.fold_in(arg_keys[4], 71), 0)
    slot_gate = jnp.clip(0.1 + 0.9 * jax.random.uniform(arg_keys[2], (SOURCES, EXPERTS, SLOT), jnp.float32) ** block_scale(arg_keys[2], (SOURCES, EXPERTS, SLOT), ((0, 32),), -0.2, 0.2), 0.1, 1.0)
    w_down = noise(arg_keys[3], (EXPERTS, F, D), F ** -0.5, 0.09375, ((0, 8), (1, 4)))
    return {"cotangent": cotangent, "slot_token": slot_token, "slot_gate": slot_gate, "w_down": w_down}


def reference(cotangent, slot_token, slot_gate, w_down):
    live_slot = slot_token >= 0
    row_base = (jnp.arange(SOURCES, dtype=jnp.int32) * TOK_DEV)[:, None, None]
    token_id = (row_base + jnp.maximum(slot_token, 0)).astype(jnp.int32)
    gate_value = jnp.where(live_slot, slot_gate, jnp.float32(0.0))
    slot_count = jnp.sum(live_slot.astype(jnp.int32), axis=2)

    def reorder(values):
        shaped = values.reshape((N_EXPERT, N_HIDDEN) + values.shape[1:])
        moved = jnp.moveaxis(jnp.moveaxis(shaped, 2, 0), 2, 1)
        return moved.reshape((EXPERTS, SOURCES) + values.shape[2:])

    token_order = reorder(token_id)
    gate_order = reorder(gate_value)
    count_order = reorder(slot_count[:, :, None])[:, :, 0]

    def one_expert(items):
        token_rows, gate_rows, count_rows, weight = items
        picked = cotangent[token_rows.reshape(-1)]
        scaled = (gate_rows.reshape(-1)[:, None] * picked.astype(jnp.float32)).astype(jnp.bfloat16)
        running = jnp.cumsum(count_rows).astype(jnp.int32)
        first_slot = running - count_rows
        row_number = jnp.arange(CAP, dtype=jnp.int32)
        source = jnp.sum((running[None, :] <= row_number[:, None]).astype(jnp.int32), axis=1).astype(jnp.int32)
        flat_index = (source * SLOT + row_number - first_slot[source]).astype(jnp.int32)
        routed = scaled[flat_index]
        return jnp.dot(routed, weight.T, preferred_element_type=jnp.float32).astype(jnp.bfloat16)

    return lax.map(one_expert, (token_order, gate_order, count_order, w_down))
```

```python
import functools

import jax
import jax.numpy as jnp
import numpy as np
from jax import lax
from jax.experimental import pallas as pl
from jax.experimental.pallas import tpu as pltpu
from jax.sharding import PartitionSpec as P

CF = 2
TILE = 256
MESH = pl.DeviceIdType.MESH


def nt_dot(a, b):
    return lax.dot_general(a, b, (((1,), (1,)), ((), ())), preferred_element_type=jnp.float32)


def kernel(
    n_ex, n_hid, slots, cot, meta_in, info, w_hbm, out_hbm,
    raw, meta, cnt, cnts, send_a, send_b, got_a, got_b, routed_b, routed_a, weight, stage,
    raw_send, raw_recv, meta_send, meta_recv, cnt_send, cnt_recv,
    a_send, a_recv, b_send, b_recv, rb_send, rb_recv, w_sem, out_sem,
):
    ex, hid = lax.axis_index("expert"), lax.axis_index("hidden")
    tokens = cot.shape[0]
    wide = raw.shape[2]
    narrow = send_b.shape[1]
    group = routed_b.shape[1]
    lanes = meta.shape[2]
    peers_rows = (n_ex - 1) * slots

    def rows_of(i):
        return pl.ds(pl.multiple_of(i * slots, 16), slots)

    barrier = pltpu.get_barrier_semaphore()

    def greet_plane(i, carry):
        pl.semaphore_signal(barrier, inc=1, device_id={"expert": lax.rem(ex + i, n_ex)}, device_id_type=MESH)
        return carry

    def greet_line(i, carry):
        pl.semaphore_signal(barrier, inc=1, device_id={"hidden": lax.rem(hid + i, n_hid)}, device_id_type=MESH)
        return carry

    lax.fori_loop(1, n_ex, greet_plane, 0)
    lax.fori_loop(1, n_hid, greet_line, 0)
    pl.semaphore_wait(barrier, n_ex + n_hid - 2)

    weight_copy = pltpu.make_async_copy(w_hbm.at[0], weight, w_sem)

    def meta_copy(i):
        return pltpu.make_async_remote_copy(
            src_ref=meta_in, dst_ref=meta.at[hid], send_sem=meta_send.at[i], recv_sem=meta_recv.at[hid],
            device_id={"hidden": lax.rem(hid + i, n_hid)}, device_id_type=MESH,
        )

    def line_copy(src, dst, send, recv, way, shard):
        return pltpu.make_async_remote_copy(
            src_ref=src, dst_ref=dst, send_sem=send.at[way, shard], recv_sem=recv.at[shard],
            device_id={"hidden": hid + 1 - 2 * way}, device_id_type=MESH,
        )

    def has_next(way):
        after = hid + 1 - 2 * way
        return (after >= 0) & (after < n_hid)

    def both_ways(body):
        def step(way, carry):
            body(way)
            return carry

        lax.fori_loop(0, 2, step, 0)

    def start_raw(way):
        @pl.when(has_next(way))
        def _():
            line_copy(cot.at[:, pl.ds(0, wide)], raw.at[hid], raw_send, raw_recv, way, hid).start()

    for i in range(1, n_hid):
        meta_copy(i).start()
    both_ways(start_raw)
    meta[hid] = meta_in[...]

    lane = lax.broadcasted_iota(jnp.int32, (slots, lanes), 1)
    token_iota = lax.broadcasted_iota(jnp.int32, (slots, tokens), 1).astype(jnp.float32)

    def choice(shard, expert):
        held = meta[shard]
        token = jnp.sum(jnp.where(lane == expert, held, 0.0), axis=1, keepdims=True)
        gate = jnp.sum(jnp.where(lane == expert + n_ex, held, 0.0), axis=1, keepdims=True)
        return jnp.where(token == token_iota, 1.0, 0.0).astype(jnp.bfloat16), gate

    def scaled(picked, gate, rows):
        return (gate * jnp.dot(picked, rows, preferred_element_type=jnp.float32)).astype(jnp.bfloat16)

    def a_copy(shard, expert):
        return pltpu.make_async_remote_copy(
            src_ref=send_a.at[shard, rows_of(expert)], dst_ref=got_a.at[shard, rows_of(ex)],
            send_sem=a_send.at[shard], recv_sem=a_recv.at[shard],
            device_id={"expert": expert}, device_id_type=MESH,
        )

    def b_copy(expert):
        return pltpu.make_async_remote_copy(
            src_ref=send_b.at[rows_of(expert)], dst_ref=got_b.at[rows_of(ex)],
            send_sem=b_send, recv_sem=b_recv, device_id={"expert": expert}, device_id_type=MESH,
        )

    def send_narrow(i, carry):
        expert = lax.rem(ex + i, n_ex)
        picked, gate = choice(hid, expert)
        send_b[rows_of(expert), :] = scaled(picked, gate, cot[:, wide:])
        b_copy(expert).start()
        return carry

    lax.fori_loop(1, n_ex, send_narrow, 0)
    picked, gate = choice(hid, ex)
    got_b[rows_of(ex), :] = scaled(picked, gate, cot[:, wide:])

    def send_wide(shard, rows):
        def one(i, carry):
            expert = lax.rem(ex + i, n_ex)
            picked, gate = choice(shard, expert)
            send_a[shard, rows_of(expert), :] = scaled(picked, gate, rows())
            a_copy(shard, expert).start()
            return carry

        lax.fori_loop(1, n_ex, one, 0)
        picked, gate = choice(shard, ex)
        got_a[shard, rows_of(ex), :] = scaled(picked, gate, rows())

    send_wide(hid, lambda: cot[:, :wide])
    weight_copy.start()

    for i in range(1, n_hid):
        source = lax.rem(hid + i, n_hid)
        pltpu.make_async_copy(meta.at[source], meta.at[source], meta_recv.at[source]).wait()
    cnt[...] = jnp.zeros(cnt.shape, cnt.dtype)
    for shard in range(n_hid):
        live = jnp.where((meta[shard] >= 0.0) & (lane < n_ex), 1.0, 0.0)
        cnt[shard : shard + 1, :] = jnp.sum(live, axis=0, keepdims=True)

    def cnt_copy(i):
        return pltpu.make_async_remote_copy(
            src_ref=cnt, dst_ref=cnts.at[ex], send_sem=cnt_send, recv_sem=cnt_recv,
            device_id={"expert": lax.rem(ex + i, n_ex)}, device_id_type=MESH,
        )

    def send_cnt(i, carry):
        cnt_copy(i).start()
        return carry

    lax.fori_loop(1, n_ex, send_cnt, 0)
    cnts[ex] = cnt[...]
    pltpu.make_async_copy(cnts.at[pl.ds(0, n_ex - 1)], cnts.at[pl.ds(0, n_ex - 1)], cnt_recv).wait()

    one_lane = lax.broadcasted_iota(jnp.int32, (1, lanes), 1)

    def order(shard):
        owner, place = info[0:1, :], info[1:2, :]

        def add(source, carry):
            first, own = carry
            row = cnts[source, pl.ds(shard, 1), :]
            count = jnp.sum(jnp.where(one_lane == ex, row, 0.0), axis=1, keepdims=True)
            at = source.astype(jnp.float32)
            return first + jnp.where(owner > at, count, 0.0), own + jnp.where(owner == at, count, 0.0)

        zero = jnp.zeros(owner.shape, jnp.float32)
        first, own = lax.fori_loop(0, n_ex, add, (zero, zero))
        target = jnp.where(place < own, first + place, -1.0)
        row = lax.broadcasted_iota(jnp.int32, (group, owner.shape[1]), 0).astype(jnp.float32)
        return jnp.where(row == target, 1.0, 0.0).astype(jnp.bfloat16)

    pltpu.make_async_copy(got_b.at[pl.ds(0, peers_rows)], got_b.at[pl.ds(0, peers_rows)], b_recv).wait()
    routed_b[hid] = jnp.dot(order(hid), got_b[...], preferred_element_type=jnp.float32).astype(jnp.bfloat16)

    def start_routed(way):
        @pl.when(has_next(way))
        def _():
            line_copy(routed_b.at[hid], routed_b.at[hid], rb_send, rb_recv, way, hid).start()

    both_ways(start_routed)

    def on_line(step, body):
        def one(way):
            shard = hid - step + 2 * step * way

            @pl.when((shard >= 0) & (shard < n_hid))
            def _():
                body(way, shard)

        both_ways(one)

    def take_raw(way, shard):
        pltpu.make_async_copy(raw.at[shard], raw.at[shard], raw_recv.at[shard]).wait()

        @pl.when(has_next(way))
        def _():
            line_copy(raw.at[shard], raw.at[shard], raw_send, raw_recv, way, shard).start()

        send_wide(shard, lambda: raw[shard])

    def take_routed(way, shard):
        pltpu.make_async_copy(routed_b.at[shard], routed_b.at[shard], rb_recv.at[shard]).wait()

        @pl.when(has_next(way))
        def _():
            line_copy(routed_b.at[shard], routed_b.at[shard], rb_send, rb_recv, way, shard).start()

    def along(step, carry):
        on_line(step, take_raw)
        on_line(step, take_routed)
        return carry

    lax.fori_loop(1, n_hid, along, 0)
    weight_copy.wait()

    def out_copy(shard):
        rows = pl.ds(pl.multiple_of(shard * group, 16), group)
        return pltpu.make_async_copy(stage.at[shard], out_hbm.at[0, rows], out_sem.at[shard])

    def finish(shard):
        @pl.when(n_ex > 1)
        def _():
            part = got_a.at[shard, pl.ds(0, peers_rows)]
            pltpu.make_async_copy(part, part, a_recv.at[shard]).wait()

        put = order(shard)

        def compact(c, carry):
            columns = pl.ds(pl.multiple_of(c * TILE, TILE), TILE)
            part = jnp.dot(put, got_a[shard, :, columns], preferred_element_type=jnp.float32)
            routed_a[:, columns] = part.astype(jnp.bfloat16)
            return carry

        lax.fori_loop(0, wide // TILE, compact, 0)

        def multiply(c, carry):
            columns = pl.ds(pl.multiple_of(c * TILE, TILE), TILE)
            total = nt_dot(routed_a[...], weight[columns, :wide]) + nt_dot(routed_b[shard], weight[columns, wide:])
            stage[shard, :, columns] = total.astype(jnp.bfloat16)
            return carry

        lax.fori_loop(0, stage.shape[2] // TILE, multiply, 0)
        out_copy(shard).start()

    def finish_step(m, carry):
        step, way = (m + 1) // 2, lax.rem(m + 1, 2)
        shard = hid - step + 2 * step * way

        @pl.when((shard >= 0) & (shard < n_hid))
        def _():
            finish(shard)

        return carry

    lax.fori_loop(0, 2 * n_hid - 1, finish_step, 0)

    for shard in range(n_hid):
        out_copy(shard).wait()
        part = send_a.at[shard, pl.ds(0, peers_rows)]
        pltpu.make_async_copy(part, part, a_send.at[shard]).wait()
        for way in range(2):
            sent = has_next(way) & ((shard <= hid) if way == 0 else (shard >= hid))

            @pl.when(sent)
            def _():
                line_copy(raw.at[shard], raw.at[shard], raw_send, raw_recv, way, shard).wait_send()
                line_copy(routed_b.at[shard], routed_b.at[shard], rb_send, rb_recv, way, shard).wait_send()

    part = send_b.at[pl.ds(0, peers_rows)]
    pltpu.make_async_copy(part, part, b_send).wait()
    pltpu.make_async_copy(cnts.at[pl.ds(0, n_ex - 1)], cnts.at[pl.ds(0, n_ex - 1)], cnt_send).wait()
    for i in range(1, n_hid):
        meta_copy(i).wait_send()


def shards(n_ex, n_hid, cotangent, slot_token, slot_gate, w_down):
    tokens, features = cotangent.shape
    hidden = w_down.shape[1]
    slots = -(-slot_token.shape[2] // 16) * 16
    lanes = -(-2 * n_ex // 128) * 128
    wide = features * 3 // 4 // TILE * TILE
    narrow = features - wide
    group = CF * tokens
    spare = ((0, slots - slot_token.shape[2]), (0, 0))
    token = jnp.pad(slot_token[0].T.astype(jnp.float32), spare, constant_values=-1.0)
    gate = jnp.pad(slot_gate[0].T, spare)
    meta = jnp.pad(jnp.concatenate([token, gate], axis=1), ((0, 0), (0, lanes - 2 * n_ex)))
    place = np.arange(n_ex * slots)
    info = np.zeros((8, n_ex * slots), np.float32)
    info[0], info[1] = place // slots, place % slots
    dma = pltpu.SemaphoreType.DMA
    bf16, f32 = jnp.bfloat16, jnp.float32
    vmem = pl.BlockSpec(memory_space=pltpu.VMEM)
    return pl.pallas_call(
        functools.partial(kernel, n_ex, n_hid, slots),
        out_shape=jax.ShapeDtypeStruct((1, n_hid * group, hidden), bf16),
        in_specs=[vmem, vmem, vmem, pl.BlockSpec(memory_space=pl.ANY)],
        out_specs=pl.BlockSpec(memory_space=pl.ANY),
        scratch_shapes=[
            pltpu.VMEM((n_hid, tokens, wide), bf16),
            pltpu.VMEM((n_hid, slots, lanes), f32),
            pltpu.VMEM((-(-n_hid // 8) * 8, lanes), f32),
            pltpu.VMEM((n_ex, -(-n_hid // 8) * 8, lanes), f32),
            pltpu.VMEM((n_hid, n_ex * slots, wide), bf16),
            pltpu.VMEM((n_ex * slots, narrow), bf16),
            pltpu.VMEM((n_hid, n_ex * slots, wide), bf16),
            pltpu.VMEM((n_ex * slots, narrow), bf16),
            pltpu.VMEM((n_hid, group, narrow), bf16),
            pltpu.VMEM((group, wide), bf16),
            pltpu.VMEM((hidden, features), bf16),
            pltpu.VMEM((n_hid, group, hidden), bf16),
            dma((2, n_hid)), dma((n_hid,)), dma((n_hid,)), dma((n_hid,)), dma, dma,
            dma((n_hid,)), dma((n_hid,)), dma, dma, dma((2, n_hid)), dma((n_hid,)), dma, dma((n_hid,)),
        ],
        compiler_params=pltpu.CompilerParams(
            collective_id=0, has_side_effects=True, vmem_limit_bytes=60 * 1024 * 1024
        ),
        cost_estimate=pl.CostEstimate(
            flops=2 * n_hid * group * hidden * features, bytes_accessed=2 * hidden * features * 3, transcendentals=0
        ),
        name="route_and_multiply",
    )(cotangent, meta, jnp.asarray(info), w_down)


def solution(mesh):
    n_ex, n_hid = mesh.shape["expert"], mesh.shape["hidden"]
    in_specs = (
        P(("expert", "hidden"), None),
        P(("expert", "hidden"), None, None),
        P(("expert", "hidden"), None, None),
        P("expert", "hidden", None),
    )
    out_specs = P("expert", None, "hidden")
    return jax.shard_map(
        functools.partial(shards, n_ex, n_hid), mesh=mesh, in_specs=in_specs, out_specs=out_specs, check_vma=False
    )
```

```python
import functools

import jax
import jax.numpy as jnp
import numpy as np
from jax import lax
from jax.experimental import pallas as pl
from jax.experimental.pallas import tpu as pltpu
from jax.sharding import PartitionSpec as P

CF = 2
TILE = 256
MESH = pl.DeviceIdType.MESH


def nt_dot(a, b):
    return lax.dot_general(a, b, (((1,), (1,)), ((), ())), preferred_element_type=jnp.float32)


def kernel(
    n_ex, n_hid, slots, cot, token_in, gate_in, info, w_hbm, stage,
    raw, table, meta, cnt, cnts, send_a, send_b, got_a, got_b, routed_b, routed_a, weight,
    raw_send, raw_recv, meta_send, meta_recv, cnt_send, cnt_recv,
    a_send, a_recv, b_send, b_recv, rb_send, rb_recv, w_sem,
):
    ex, hid = lax.axis_index("expert"), lax.axis_index("hidden")
    tokens = cot.shape[0]
    wide = raw.shape[2]
    narrow = send_b.shape[1]
    group = routed_b.shape[1]
    lanes = meta.shape[2]
    peers_rows = (n_ex - 1) * slots

    def rows_of(i):
        return pl.ds(pl.multiple_of(i * slots, 16), slots)

    barrier = pltpu.get_barrier_semaphore()

    def greet_plane(i, carry):
        pl.semaphore_signal(barrier, inc=1, device_id={"expert": lax.rem(ex + i, n_ex)}, device_id_type=MESH)
        return carry

    def greet_line(i, carry):
        pl.semaphore_signal(barrier, inc=1, device_id={"hidden": lax.rem(hid + i, n_hid)}, device_id_type=MESH)
        return carry

    lax.fori_loop(1, n_ex, greet_plane, 0)
    lax.fori_loop(1, n_hid, greet_line, 0)
    pl.semaphore_wait(barrier, n_ex + n_hid - 2)

    weight_copy = pltpu.make_async_copy(w_hbm.at[0], weight, w_sem)

    def meta_copy(i):
        return pltpu.make_async_remote_copy(
            src_ref=meta.at[hid], dst_ref=meta.at[hid], send_sem=meta_send.at[i], recv_sem=meta_recv.at[hid],
            device_id={"hidden": lax.rem(hid + i, n_hid)}, device_id_type=MESH,
        )

    def line_copy(src, dst, send, recv, way, shard):
        return pltpu.make_async_remote_copy(
            src_ref=src, dst_ref=dst, send_sem=send.at[way, shard], recv_sem=recv.at[shard],
            device_id={"hidden": hid + 1 - 2 * way}, device_id_type=MESH,
        )

    def has_next(way):
        after = hid + 1 - 2 * way
        return (after >= 0) & (after < n_hid)

    def both_ways(body):
        def step(way, carry):
            body(way)
            return carry

        lax.fori_loop(0, 2, step, 0)

    def start_raw(way):
        @pl.when(has_next(way))
        def _():
            line_copy(cot.at[:, pl.ds(0, wide)], raw.at[hid], raw_send, raw_recv, way, hid).start()

    both_ways(start_raw)
    live_slots = token_in.shape[2]
    table[...] = jnp.where(lax.broadcasted_iota(jnp.int32, table.shape, 0) < n_ex, -1.0, 0.0)
    table[0:n_ex, 0:live_slots] = token_in[0].astype(jnp.float32)
    table[n_ex : 2 * n_ex, 0:live_slots] = gate_in[0]
    meta[hid] = table[...].T[0:slots, :]
    for i in range(1, n_hid):
        meta_copy(i).start()

    lane = lax.broadcasted_iota(jnp.int32, (slots, lanes), 1)
    token_iota = lax.broadcasted_iota(jnp.int32, (slots, tokens), 1).astype(jnp.float32)

    def choice(shard, expert):
        held = meta[shard]
        token = jnp.sum(jnp.where(lane == expert, held, 0.0), axis=1, keepdims=True)
        gate = jnp.sum(jnp.where(lane == expert + n_ex, held, 0.0), axis=1, keepdims=True)
        return jnp.where(token == token_iota, 1.0, 0.0).astype(jnp.bfloat16), gate

    def scaled(picked, gate, rows):
        return (gate * jnp.dot(picked, rows, preferred_element_type=jnp.float32)).astype(jnp.bfloat16)

    def a_copy(shard, expert):
        return pltpu.make_async_remote_copy(
            src_ref=send_a.at[shard, rows_of(expert)], dst_ref=got_a.at[shard, rows_of(ex)],
            send_sem=a_send.at[shard], recv_sem=a_recv.at[shard],
            device_id={"expert": expert}, device_id_type=MESH,
        )

    def b_copy(expert):
        return pltpu.make_async_remote_copy(
            src_ref=send_b.at[rows_of(expert)], dst_ref=got_b.at[rows_of(ex)],
            send_sem=b_send, recv_sem=b_recv, device_id={"expert": expert}, device_id_type=MESH,
        )

    def send_narrow(i, carry):
        expert = lax.rem(ex + i, n_ex)
        picked, gate = choice(hid, expert)
        send_b[rows_of(expert), :] = scaled(picked, gate, cot[:, wide:])
        b_copy(expert).start()
        return carry

    lax.fori_loop(1, n_ex, send_narrow, 0)
    picked, gate = choice(hid, ex)
    got_b[rows_of(ex), :] = scaled(picked, gate, cot[:, wide:])

    def send_wide(shard, rows):
        def one(i, carry):
            expert = lax.rem(ex + i, n_ex)
            picked, gate = choice(shard, expert)
            send_a[shard, rows_of(expert), :] = scaled(picked, gate, rows())
            a_copy(shard, expert).start()
            return carry

        lax.fori_loop(1, n_ex, one, 0)
        picked, gate = choice(shard, ex)
        got_a[shard, rows_of(ex), :] = scaled(picked, gate, rows())

    send_wide(hid, lambda: cot[:, :wide])
    weight_copy.start()

    for i in range(1, n_hid):
        source = lax.rem(hid + i, n_hid)
        pltpu.make_async_copy(meta.at[source], meta.at[source], meta_recv.at[source]).wait()
    cnt[...] = jnp.zeros(cnt.shape, cnt.dtype)
    for shard in range(n_hid):
        live = jnp.where((meta[shard] >= 0.0) & (lane < n_ex), 1.0, 0.0)
        cnt[shard : shard + 1, :] = jnp.sum(live, axis=0, keepdims=True)

    def cnt_copy(i):
        return pltpu.make_async_remote_copy(
            src_ref=cnt, dst_ref=cnts.at[ex], send_sem=cnt_send, recv_sem=cnt_recv,
            device_id={"expert": lax.rem(ex + i, n_ex)}, device_id_type=MESH,
        )

    def send_cnt(i, carry):
        cnt_copy(i).start()
        return carry

    lax.fori_loop(1, n_ex, send_cnt, 0)
    cnts[ex] = cnt[...]
    pltpu.make_async_copy(cnts.at[pl.ds(0, n_ex - 1)], cnts.at[pl.ds(0, n_ex - 1)], cnt_recv).wait()

    one_lane = lax.broadcasted_iota(jnp.int32, (1, lanes), 1)

    def order(shard):
        owner, place = info[0:1, :], info[1:2, :]

        def add(source, carry):
            first, own = carry
            row = cnts[source, pl.ds(shard, 1), :]
            count = jnp.sum(jnp.where(one_lane == ex, row, 0.0), axis=1, keepdims=True)
            at = source.astype(jnp.float32)
            return first + jnp.where(owner > at, count, 0.0), own + jnp.where(owner == at, count, 0.0)

        zero = jnp.zeros(owner.shape, jnp.float32)
        first, own = lax.fori_loop(0, n_ex, add, (zero, zero))
        target = jnp.where(place < own, first + place, -1.0)
        row = lax.broadcasted_iota(jnp.int32, (group, owner.shape[1]), 0).astype(jnp.float32)
        return jnp.where(row == target, 1.0, 0.0).astype(jnp.bfloat16)

    pltpu.make_async_copy(got_b.at[pl.ds(0, peers_rows)], got_b.at[pl.ds(0, peers_rows)], b_recv).wait()
    routed_b[hid] = jnp.dot(order(hid), got_b[...], preferred_element_type=jnp.float32).astype(jnp.bfloat16)

    def start_routed(way):
        @pl.when(has_next(way))
        def _():
            line_copy(routed_b.at[hid], routed_b.at[hid], rb_send, rb_recv, way, hid).start()

    def on_line(step, body):
        def one(way):
            shard = hid - step + 2 * step * way

            @pl.when((shard >= 0) & (shard < n_hid))
            def _():
                body(way, shard)

        both_ways(one)

    def take_raw(way, shard):
        pltpu.make_async_copy(raw.at[shard], raw.at[shard], raw_recv.at[shard]).wait()

        @pl.when(has_next(way))
        def _():
            line_copy(raw.at[shard], raw.at[shard], raw_send, raw_recv, way, shard).start()

        send_wide(shard, lambda: raw[shard])

    def take_routed(way, shard):
        pltpu.make_async_copy(routed_b.at[shard], routed_b.at[shard], rb_recv.at[shard]).wait()

        @pl.when(has_next(way))
        def _():
            line_copy(routed_b.at[shard], routed_b.at[shard], rb_send, rb_recv, way, shard).start()

    def along(step, carry):
        on_line(step, take_raw)
        last_raw(step)
        return carry

    def last_raw(step):
        def one(way):
            @pl.when(step == hid + way * (n_hid - 1 - 2 * hid))
            def _():
                start_routed(way)

        both_ways(one)

    last_raw(0)
    lax.fori_loop(1, n_hid, along, 0)

    def along_routed(step, carry):
        on_line(step, take_routed)
        return carry

    lax.fori_loop(1, n_hid, along_routed, 0)
    weight_copy.wait()

    def finish(shard):
        @pl.when(n_ex > 1)
        def _():
            part = got_a.at[shard, pl.ds(0, peers_rows)]
            pltpu.make_async_copy(part, part, a_recv.at[shard]).wait()

        put = order(shard)

        def compact(c, carry):
            columns = pl.ds(pl.multiple_of(c * TILE, TILE), TILE)
            part = jnp.dot(put, got_a[shard, :, columns], preferred_element_type=jnp.float32)
            routed_a[:, columns] = part.astype(jnp.bfloat16)
            return carry

        lax.fori_loop(0, wide // TILE, compact, 0)

        def multiply(c, carry):
            columns = pl.ds(pl.multiple_of(c * TILE, TILE), TILE)
            total = nt_dot(routed_a[...], weight[columns, :wide]) + nt_dot(routed_b[shard], weight[columns, wide:])
            stage[0, rows, columns] = total.astype(jnp.bfloat16)
            return carry

        rows = pl.ds(pl.multiple_of(shard * group, 16), group)
        lax.fori_loop(0, stage.shape[2] // TILE, multiply, 0)

    def finish_step(m, carry):
        step, way = (m + 1) // 2, lax.rem(m + 1, 2)
        shard = hid - step + 2 * step * way

        @pl.when((shard >= 0) & (shard < n_hid))
        def _():
            finish(shard)

        return carry

    lax.fori_loop(0, 2 * n_hid - 1, finish_step, 0)

    for shard in range(n_hid):
        part = send_a.at[shard, pl.ds(0, peers_rows)]
        pltpu.make_async_copy(part, part, a_send.at[shard]).wait()
        for way in range(2):
            sent = has_next(way) & ((shard <= hid) if way == 0 else (shard >= hid))

            @pl.when(sent)
            def _():
                line_copy(raw.at[shard], raw.at[shard], raw_send, raw_recv, way, shard).wait_send()
                line_copy(routed_b.at[shard], routed_b.at[shard], rb_send, rb_recv, way, shard).wait_send()

    part = send_b.at[pl.ds(0, peers_rows)]
    pltpu.make_async_copy(part, part, b_send).wait()
    pltpu.make_async_copy(cnts.at[pl.ds(0, n_ex - 1)], cnts.at[pl.ds(0, n_ex - 1)], cnt_send).wait()
    for i in range(1, n_hid):
        meta_copy(i).wait_send()


def shards(n_ex, n_hid, cotangent, slot_token, slot_gate, w_down):
    tokens, features = cotangent.shape
    hidden = w_down.shape[1]
    slots = -(-slot_token.shape[2] // 16) * 16
    lanes = -(-2 * n_ex // 128) * 128
    wide = features * 3 // 4 // TILE * TILE
    narrow = features - wide
    group = CF * tokens
    place = np.arange(n_ex * slots)
    info = np.zeros((8, n_ex * slots), np.float32)
    info[0], info[1] = place // slots, place % slots
    dma = pltpu.SemaphoreType.DMA
    bf16, f32 = jnp.bfloat16, jnp.float32
    vmem = pl.BlockSpec(memory_space=pltpu.VMEM)
    return pl.pallas_call(
        functools.partial(kernel, n_ex, n_hid, slots),
        out_shape=pltpu.VMEM((1, n_hid * group, hidden), bf16),
        in_specs=[vmem, vmem, vmem, vmem, pl.BlockSpec(memory_space=pl.ANY)],
        out_specs=vmem,
        scratch_shapes=[
            pltpu.VMEM((n_hid, tokens, wide), bf16),
            pltpu.VMEM((lanes, 128), f32),
            pltpu.VMEM((n_hid, slots, lanes), f32),
            pltpu.VMEM((-(-n_hid // 8) * 8, lanes), f32),
            pltpu.VMEM((n_ex, -(-n_hid // 8) * 8, lanes), f32),
            pltpu.VMEM((n_hid, n_ex * slots, wide), bf16),
            pltpu.VMEM((n_ex * slots, narrow), bf16),
            pltpu.VMEM((n_hid, n_ex * slots, wide), bf16),
            pltpu.VMEM((n_ex * slots, narrow), bf16),
            pltpu.VMEM((n_hid, group, narrow), bf16),
            pltpu.VMEM((group, wide), bf16),
            pltpu.VMEM((hidden, features), bf16),
            dma((2, n_hid)), dma((n_hid,)), dma((n_hid,)), dma((n_hid,)), dma, dma,
            dma((n_hid,)), dma((n_hid,)), dma, dma, dma((2, n_hid)), dma((n_hid,)), dma,
        ],
        compiler_params=pltpu.CompilerParams(
            collective_id=0, has_side_effects=True, vmem_limit_bytes=48 * 1024 * 1024
        ),
        cost_estimate=pl.CostEstimate(
            flops=2 * n_hid * group * hidden * features, bytes_accessed=2 * hidden * features * 3, transcendentals=0
        ),
        name="route_and_multiply",
    )(cotangent, slot_token, slot_gate, jnp.asarray(info), w_down)


def solution(mesh):
    n_ex, n_hid = mesh.shape["expert"], mesh.shape["hidden"]
    in_specs = (
        P(("expert", "hidden"), None),
        P(("expert", "hidden"), None, None),
        P(("expert", "hidden"), None, None),
        P("expert", "hidden", None),
    )
    out_specs = P("expert", None, "hidden")
    return jax.shard_map(
        functools.partial(shards, n_ex, n_hid), mesh=mesh, in_specs=in_specs, out_specs=out_specs, check_vma=False
    )
```

```python
import functools

import jax
import jax.numpy as jnp
from jax import lax
from jax.experimental import pallas as pl
from jax.experimental.pallas import tpu as pltpu
from jax.sharding import PartitionSpec as P

CF = 2
TILE = 256
MESH = pl.DeviceIdType.MESH


def kernel(
    n_ex, n_hid, slots, cot_hbm, token_hbm, gate_hbm, w_hbm, stage,
    cot, token_in, gate_in, pick, gates, put, weight_t,
    raw, table, meta, cnt, cnts, send_a, send_b, got_a, got_b, routed_b, routed_a, weight,
    raw_send, raw_recv, meta_send, meta_recv, cnt_send, cnt_recv,
    a_send, a_recv, b_send, b_recv, rb_send, rb_recv, load_sem,
):
    ex, hid = lax.axis_index("expert"), lax.axis_index("hidden")
    tokens = cot.shape[0]
    wide = raw.shape[2]
    narrow = send_b.shape[1]
    group = routed_b.shape[1]
    lanes = meta.shape[2]
    peers_rows = (n_ex - 1) * slots

    def rows_of(i):
        return pl.ds(pl.multiple_of(i * slots, 16), slots)

    loads = [
        pltpu.make_async_copy(source, target, load_sem.at[i])
        for i, (source, target) in enumerate(
            [(token_hbm, token_in), (gate_hbm, gate_in), (cot_hbm, cot), (w_hbm.at[0], weight)]
        )
    ]
    for load in loads:
        load.start()

    barrier = pltpu.get_barrier_semaphore()

    def greet_plane(i, carry):
        pl.semaphore_signal(barrier, inc=1, device_id={"expert": lax.rem(ex + i, n_ex)}, device_id_type=MESH)
        return carry

    def greet_line(i, carry):
        pl.semaphore_signal(barrier, inc=1, device_id={"hidden": lax.rem(hid + i, n_hid)}, device_id_type=MESH)
        return carry

    lax.fori_loop(1, n_ex, greet_plane, 0)
    lax.fori_loop(1, n_hid, greet_line, 0)
    pl.semaphore_wait(barrier, n_ex + n_hid - 2)

    def meta_copy(i):
        return pltpu.make_async_remote_copy(
            src_ref=meta.at[hid], dst_ref=meta.at[hid], send_sem=meta_send.at[i], recv_sem=meta_recv.at[hid],
            device_id={"hidden": lax.rem(hid + i, n_hid)}, device_id_type=MESH,
        )

    def line_copy(src, dst, send, recv, way, shard):
        return pltpu.make_async_remote_copy(
            src_ref=src, dst_ref=dst, send_sem=send.at[way, shard], recv_sem=recv.at[shard],
            device_id={"hidden": hid + 1 - 2 * way}, device_id_type=MESH,
        )

    def has_next(way):
        after = hid + 1 - 2 * way
        return (after >= 0) & (after < n_hid)

    def both_ways(body):
        def step(way, carry):
            body(way)
            return carry

        lax.fori_loop(0, 2, step, 0)

    def start_raw(way):
        @pl.when(has_next(way))
        def _():
            line_copy(cot_hbm.at[:, pl.ds(0, wide)], raw.at[hid], raw_send, raw_recv, way, hid).start()

    both_ways(start_raw)
    loads[0].wait()
    loads[1].wait()
    live_slots = token_in.shape[2]
    table[...] = jnp.where(lax.broadcasted_iota(jnp.int32, table.shape, 0) < n_ex, -1.0, 0.0)
    table[0:n_ex, 0:live_slots] = token_in[0].astype(jnp.float32)
    table[n_ex : 2 * n_ex, 0:live_slots] = gate_in[0]
    meta[hid] = table[...].T[0:slots, :]
    for i in range(1, n_hid):
        meta_copy(i).start()

    lane = lax.broadcasted_iota(jnp.int32, (slots, lanes), 1)
    token_iota = lax.broadcasted_iota(jnp.int32, (slots, tokens), 1).astype(jnp.float32)

    def choose(shard):
        held = meta[shard]

        def one(expert, carry):
            token = jnp.sum(jnp.where(lane == expert, held, 0.0), axis=1, keepdims=True)
            gate = jnp.sum(jnp.where(lane == expert + n_ex, held, 0.0), axis=1, keepdims=True)
            pick[rows_of(expert), :] = jnp.where(token == token_iota, 1.0, 0.0).astype(jnp.bfloat16)
            gates[rows_of(expert), :] = jnp.broadcast_to(gate, (slots, TILE))
            return carry

        lax.fori_loop(0, n_ex, one, 0)

    def scale(rows, store, columns):
        def one(c, carry):
            part = jnp.dot(pick[...], rows(c), preferred_element_type=jnp.float32)
            store(c, (gates[...] * part).astype(jnp.bfloat16))
            return carry

        lax.fori_loop(0, columns // TILE, one, 0)

    def tile(c, base=0):
        return pl.ds(pl.multiple_of(base + c * TILE, TILE), TILE)

    def a_copy(shard, expert):
        return pltpu.make_async_remote_copy(
            src_ref=send_a.at[shard, rows_of(expert)], dst_ref=got_a.at[shard, rows_of(ex)],
            send_sem=a_send.at[shard], recv_sem=a_recv.at[shard],
            device_id={"expert": expert}, device_id_type=MESH,
        )

    def b_copy(expert):
        return pltpu.make_async_remote_copy(
            src_ref=send_b.at[rows_of(expert)], dst_ref=got_b.at[rows_of(ex)],
            send_sem=b_send, recv_sem=b_recv, device_id={"expert": expert}, device_id_type=MESH,
        )

    def store_narrow(c, part):
        send_b[:, tile(c)] = part

    def start_narrow(i, carry):
        b_copy(lax.rem(ex + i, n_ex)).start()
        return carry

    choose(hid)
    loads[2].wait()
    scale(lambda c: cot[:, tile(c, wide)], store_narrow, narrow)
    lax.fori_loop(1, n_ex, start_narrow, 0)
    got_b[rows_of(ex), :] = send_b[rows_of(ex), :]

    def send_wide(shard, rows):
        def store_wide(c, part):
            send_a[shard, :, tile(c)] = part

        def start_wide(i, carry):
            a_copy(shard, lax.rem(ex + i, n_ex)).start()
            return carry

        scale(rows, store_wide, wide)
        lax.fori_loop(1, n_ex, start_wide, 0)
        got_a[shard, rows_of(ex), :] = send_a[shard, rows_of(ex), :]

    send_wide(hid, lambda c: cot[:, tile(c)])

    for i in range(1, n_hid):
        source = lax.rem(hid + i, n_hid)
        pltpu.make_async_copy(meta.at[source], meta.at[source], meta_recv.at[source]).wait()
    cnt[...] = jnp.zeros(cnt.shape, cnt.dtype)
    for shard in range(n_hid):
        live = jnp.where((meta[shard] >= 0.0) & (lane < n_ex), 1.0, 0.0)
        cnt[shard : shard + 1, :] = jnp.sum(live, axis=0, keepdims=True)

    def cnt_copy(i):
        return pltpu.make_async_remote_copy(
            src_ref=cnt, dst_ref=cnts.at[ex], send_sem=cnt_send, recv_sem=cnt_recv,
            device_id={"expert": lax.rem(ex + i, n_ex)}, device_id_type=MESH,
        )

    def send_cnt(i, carry):
        cnt_copy(i).start()
        return carry

    lax.fori_loop(1, n_ex, send_cnt, 0)
    cnts[ex] = cnt[...]
    pltpu.make_async_copy(cnts.at[pl.ds(0, n_ex - 1)], cnts.at[pl.ds(0, n_ex - 1)], cnt_recv).wait()

    one_lane = lax.broadcasted_iota(jnp.int32, (1, lanes), 1)

    def order(shard):
        number = lax.broadcasted_iota(jnp.int32, (1, n_ex * slots), 1).astype(jnp.float32)
        owner = jnp.floor((number + 0.5) / slots)
        place = number - owner * slots

        def add(source, carry):
            first, own = carry
            row = cnts[source, pl.ds(shard, 1), :]
            count = jnp.sum(jnp.where(one_lane == ex, row, 0.0), axis=1, keepdims=True)
            at = source.astype(jnp.float32)
            return first + jnp.where(owner > at, count, 0.0), own + jnp.where(owner == at, count, 0.0)

        zero = jnp.zeros(owner.shape, jnp.float32)
        first, own = lax.fori_loop(0, n_ex, add, (zero, zero))
        target = jnp.where(place < own, first + place, -1.0)
        row = lax.broadcasted_iota(jnp.int32, (group, owner.shape[1]), 0).astype(jnp.float32)
        put[shard] = jnp.where(row == target, 1.0, 0.0).astype(jnp.bfloat16)

    order(hid)

    pltpu.make_async_copy(got_b.at[pl.ds(0, peers_rows)], got_b.at[pl.ds(0, peers_rows)], b_recv).wait()
    routed_b[hid] = jnp.dot(put[hid], got_b[...], preferred_element_type=jnp.float32).astype(jnp.bfloat16)

    def start_routed(way):
        @pl.when(has_next(way))
        def _():
            line_copy(routed_b.at[hid], routed_b.at[hid], rb_send, rb_recv, way, hid).start()

    def on_line(step, body):
        def one(way):
            shard = hid - step + 2 * step * way

            @pl.when((shard >= 0) & (shard < n_hid))
            def _():
                body(way, shard)

        both_ways(one)

    def take_raw(way, shard):
        pltpu.make_async_copy(raw.at[shard], raw.at[shard], raw_recv.at[shard]).wait()

        @pl.when(has_next(way))
        def _():
            line_copy(raw.at[shard], raw.at[shard], raw_send, raw_recv, way, shard).start()

        choose(shard)
        send_wide(shard, lambda c: raw[shard, :, tile(c)])

    def take_routed(way, shard):
        pltpu.make_async_copy(routed_b.at[shard], routed_b.at[shard], rb_recv.at[shard]).wait()

        @pl.when(has_next(way))
        def _():
            line_copy(routed_b.at[shard], routed_b.at[shard], rb_send, rb_recv, way, shard).start()

    def along(step, carry):
        on_line(step, take_raw)
        last_raw(step)
        return carry

    def last_raw(step):
        def one(way):
            @pl.when(step == hid + way * (n_hid - 1 - 2 * hid))
            def _():
                start_routed(way)

        both_ways(one)

    last_raw(0)

    def order_other(i, carry):
        order(lax.rem(hid + i, n_hid))
        return carry

    lax.fori_loop(1, n_hid, order_other, 0)
    loads[3].wait()

    def turn(c, carry):
        weight_t[:, tile(c)] = weight[tile(c), :].T
        return carry

    lax.fori_loop(0, weight.shape[0] // TILE, turn, 0)
    lax.fori_loop(1, n_hid, along, 0)

    def finish(shard):
        @pl.when(n_ex > 1)
        def _():
            part = got_a.at[shard, pl.ds(0, peers_rows)]
            pltpu.make_async_copy(part, part, a_recv.at[shard]).wait()

        def compact(c, carry):
            columns = pl.ds(pl.multiple_of(c * TILE, TILE), TILE)
            part = jnp.dot(put[shard], got_a[shard, :, columns], preferred_element_type=jnp.float32)
            routed_a[:, columns] = part.astype(jnp.bfloat16)
            return carry

        lax.fori_loop(0, wide // TILE, compact, 0)

        def multiply(c, carry):
            columns = pl.ds(pl.multiple_of(c * TILE, TILE), TILE)
            total = jnp.dot(routed_a[...], weight_t[:wide, columns], preferred_element_type=jnp.float32)
            total += jnp.dot(routed_b[shard], weight_t[wide:, columns], preferred_element_type=jnp.float32)
            stage[0, rows, columns] = total.astype(jnp.bfloat16)
            return carry

        rows = pl.ds(pl.multiple_of(shard * group, 16), group)
        lax.fori_loop(0, stage.shape[2] // TILE, multiply, 0)

    def along_routed(step, carry):
        @pl.when(step > 0)
        def _():
            on_line(step, take_routed)

        def one(way, inner):
            shard = hid - step + 2 * step * way

            @pl.when((shard >= 0) & (shard < n_hid))
            def _():
                finish(shard)

            return inner

        lax.fori_loop(0, jnp.where(step > 0, 2, 1), one, 0)
        return carry

    lax.fori_loop(0, n_hid, along_routed, 0)

    for shard in range(n_hid):
        part = send_a.at[shard, pl.ds(0, peers_rows)]
        pltpu.make_async_copy(part, part, a_send.at[shard]).wait()
        for way in range(2):
            sent = has_next(way) & ((shard <= hid) if way == 0 else (shard >= hid))

            @pl.when(sent)
            def _():
                line_copy(raw.at[shard], raw.at[shard], raw_send, raw_recv, way, shard).wait_send()
                line_copy(routed_b.at[shard], routed_b.at[shard], rb_send, rb_recv, way, shard).wait_send()

    part = send_b.at[pl.ds(0, peers_rows)]
    pltpu.make_async_copy(part, part, b_send).wait()
    pltpu.make_async_copy(cnts.at[pl.ds(0, n_ex - 1)], cnts.at[pl.ds(0, n_ex - 1)], cnt_send).wait()
    for i in range(1, n_hid):
        meta_copy(i).wait_send()


def shards(n_ex, n_hid, cotangent, slot_token, slot_gate, w_down):
    tokens, features = cotangent.shape
    hidden = w_down.shape[1]
    slots = -(-slot_token.shape[2] // 16) * 16
    lanes = -(-2 * n_ex // 128) * 128
    wide = features * 3 // 4 // TILE * TILE
    narrow = features - wide
    group = CF * tokens
    dma = pltpu.SemaphoreType.DMA
    bf16, f32 = jnp.bfloat16, jnp.float32
    hbm = pl.BlockSpec(memory_space=pltpu.HBM)
    return pl.pallas_call(
        functools.partial(kernel, n_ex, n_hid, slots),
        out_shape=pltpu.VMEM((1, n_hid * group, hidden), bf16),
        in_specs=[hbm, hbm, hbm, hbm],
        out_specs=pl.BlockSpec(memory_space=pltpu.VMEM),
        scratch_shapes=[
            pltpu.VMEM(cotangent.shape, bf16),
            pltpu.VMEM(slot_token.shape, jnp.int32),
            pltpu.VMEM(slot_gate.shape, f32),
            pltpu.VMEM((n_ex * slots, tokens), bf16),
            pltpu.VMEM((n_ex * slots, TILE), f32),
            pltpu.VMEM((n_hid, group, n_ex * slots), bf16),
            pltpu.VMEM((features, hidden), bf16),
            pltpu.VMEM((n_hid, tokens, wide), bf16),
            pltpu.VMEM((lanes, 128), f32),
            pltpu.VMEM((n_hid, slots, lanes), f32),
            pltpu.VMEM((-(-n_hid // 8) * 8, lanes), f32),
            pltpu.VMEM((n_ex, -(-n_hid // 8) * 8, lanes), f32),
            pltpu.VMEM((n_hid, n_ex * slots, wide), bf16),
            pltpu.VMEM((n_ex * slots, narrow), bf16),
            pltpu.VMEM((n_hid, n_ex * slots, wide), bf16),
            pltpu.VMEM((n_ex * slots, narrow), bf16),
            pltpu.VMEM((n_hid, group, narrow), bf16),
            pltpu.VMEM((group, wide), bf16),
            pltpu.VMEM((hidden, features), bf16),
            dma((2, n_hid)), dma((n_hid,)), dma((n_hid,)), dma((n_hid,)), dma, dma,
            dma((n_hid,)), dma((n_hid,)), dma, dma, dma((2, n_hid)), dma((n_hid,)), dma((4,)),
        ],
        compiler_params=pltpu.CompilerParams(
            collective_id=0, has_side_effects=True, vmem_limit_bytes=52 * 1024 * 1024
        ),
        cost_estimate=pl.CostEstimate(
            flops=2 * n_hid * group * hidden * features, bytes_accessed=2 * hidden * features * 3, transcendentals=0
        ),
        name="route_and_multiply",
    )(cotangent, slot_token, slot_gate, w_down)


def solution(mesh):
    n_ex, n_hid = mesh.shape["expert"], mesh.shape["hidden"]
    in_specs = (
        P(("expert", "hidden"), None),
        P(("expert", "hidden"), None, None),
        P(("expert", "hidden"), None, None),
        P("expert", "hidden", None),
    )
    out_specs = P("expert", None, "hidden")
    return jax.shard_map(
        functools.partial(shards, n_ex, n_hid), mesh=mesh, in_specs=in_specs, out_specs=out_specs, check_vma=False
    )
```

```python
import functools

import jax
import jax.numpy as jnp
from jax import lax
from jax.experimental import pallas as pl
from jax.experimental.pallas import tpu as pltpu
from jax.sharding import PartitionSpec as P

CF = 2
CHUNKS = 2
TILE = 256
MESH = pl.DeviceIdType.MESH


def kernel(
    n_ex, n_hid, slots, cot_hbm, token_hbm, gate_hbm, w_hbm, stage,
    cot, token_in, gate_in, pick, gates, put, weight_t, total,
    raw, table, meta, cnt, cnts, send_a, send_b, got_a, got_b, routed_b, routed_a, weight,
    raw_send, raw_recv, meta_send, meta_recv, cnt_send, cnt_recv,
    a_send, a_recv, b_send, b_recv, rb_send, rb_recv, load_sem,
):
    ex, hid = lax.axis_index("expert"), lax.axis_index("hidden")
    tokens = cot.shape[0]
    part = raw.shape[3]
    wide = CHUNKS * part
    narrow = send_b.shape[1]
    group = routed_b.shape[1]
    lanes = meta.shape[2]
    peers_rows = (n_ex - 1) * slots

    def rows_of(i):
        return pl.ds(pl.multiple_of(i * slots, 16), slots)

    loads = [
        pltpu.make_async_copy(source, target, load_sem.at[i])
        for i, (source, target) in enumerate(
            [(token_hbm, token_in), (gate_hbm, gate_in), (cot_hbm, cot)]
        )
    ]
    for load in loads:
        load.start()

    def weight_load(c):
        rows = pl.ds(c * TILE, TILE)
        return pltpu.make_async_copy(w_hbm.at[0, rows], weight.at[c % 2], load_sem.at[3 + c % 2])

    w_tiles = w_hbm.shape[1] // TILE
    for c in range(min(2, w_tiles)):
        weight_load(c).start()

    barrier = pltpu.get_barrier_semaphore()

    def greet_plane(i, carry):
        pl.semaphore_signal(barrier, inc=1, device_id={"expert": lax.rem(ex + i, n_ex)}, device_id_type=MESH)
        return carry

    def greet_line(i, carry):
        pl.semaphore_signal(barrier, inc=1, device_id={"hidden": lax.rem(hid + i, n_hid)}, device_id_type=MESH)
        return carry

    lax.fori_loop(1, n_ex, greet_plane, 0)
    lax.fori_loop(1, n_hid, greet_line, 0)
    pl.semaphore_wait(barrier, n_ex + n_hid - 2)

    def meta_copy(i):
        return pltpu.make_async_remote_copy(
            src_ref=meta.at[hid], dst_ref=meta.at[hid], send_sem=meta_send.at[i], recv_sem=meta_recv.at[hid],
            device_id={"hidden": lax.rem(hid + i, n_hid)}, device_id_type=MESH,
        )

    def to_next(src, dst, send, recv, way):
        return pltpu.make_async_remote_copy(
            src_ref=src, dst_ref=dst, send_sem=send, recv_sem=recv,
            device_id={"hidden": hid + 1 - 2 * way}, device_id_type=MESH,
        )

    def raw_copy(way, shard, chunk, own=False):
        held = raw.at[shard, chunk]
        src = cot_hbm.at[:, pl.ds(chunk * part, part)] if own else held
        return to_next(src, held, raw_send.at[way, shard, chunk], raw_recv.at[shard, chunk], way)

    def routed_copy(way, shard):
        held = routed_b.at[shard]
        return to_next(held, held, rb_send.at[way, shard], rb_recv.at[shard], way)

    def has_next(way):
        after = hid + 1 - 2 * way
        return (after >= 0) & (after < n_hid)

    def both_ways(body):
        def step(way, carry):
            body(way)
            return carry

        lax.fori_loop(0, 2, step, 0)

    def start_raw(way, chunk):
        @pl.when(has_next(way))
        def _():
            raw_copy(way, hid, chunk, own=True).start()

    for chunk in range(CHUNKS):
        both_ways(functools.partial(start_raw, chunk=chunk))
    loads[0].wait()
    loads[1].wait()
    live_slots = token_in.shape[2]
    table[...] = jnp.where(lax.broadcasted_iota(jnp.int32, table.shape, 0) < n_ex, -1.0, 0.0)
    table[0:n_ex, 0:live_slots] = token_in[0].astype(jnp.float32)
    table[n_ex : 2 * n_ex, 0:live_slots] = gate_in[0]
    meta[hid] = table[...].T[0:slots, :]
    for i in range(1, n_hid):
        meta_copy(i).start()

    lane = lax.broadcasted_iota(jnp.int32, (slots, lanes), 1)
    token_iota = lax.broadcasted_iota(jnp.int32, (slots, tokens), 1).astype(jnp.float32)

    def choose(shard):
        held = meta[shard]

        def one(expert, carry):
            token = jnp.sum(jnp.where(lane == expert, held, 0.0), axis=1, keepdims=True)
            gate = jnp.sum(jnp.where(lane == expert + n_ex, held, 0.0), axis=1, keepdims=True)
            pick[shard, rows_of(expert), :] = jnp.where(token == token_iota, 1.0, 0.0).astype(jnp.bfloat16)
            gates[shard, rows_of(expert), :] = jnp.broadcast_to(gate, (slots, 128))
            return carry

        lax.fori_loop(0, n_ex, one, 0)

    def scale(shard, rows, store, columns):
        def one(c, carry):
            rows_c = jnp.dot(pick[shard], rows(c), preferred_element_type=jnp.float32)
            gate = jnp.concatenate([gates[shard]] * (TILE // 128), axis=1)
            store(c, (gate * rows_c).astype(jnp.bfloat16))
            return carry

        lax.fori_loop(0, columns // TILE, one, 0)

    def tile(c, base=0):
        return pl.ds(pl.multiple_of(base + c * TILE, TILE), TILE)

    def a_copy(shard, chunk, expert):
        return pltpu.make_async_remote_copy(
            src_ref=send_a.at[shard, chunk, rows_of(expert)], dst_ref=got_a.at[shard, chunk, rows_of(ex)],
            send_sem=a_send.at[shard, chunk], recv_sem=a_recv.at[shard, chunk],
            device_id={"expert": expert}, device_id_type=MESH,
        )

    def b_copy(expert):
        return pltpu.make_async_remote_copy(
            src_ref=send_b.at[rows_of(expert)], dst_ref=got_b.at[rows_of(ex)],
            send_sem=b_send, recv_sem=b_recv, device_id={"expert": expert}, device_id_type=MESH,
        )

    def store_narrow(c, value):
        send_b[:, tile(c)] = value

    def start_narrow(i, carry):
        b_copy(lax.rem(ex + i, n_ex)).start()
        return carry

    choose(hid)
    loads[2].wait()
    scale(hid, lambda c: cot[:, tile(c, wide)], store_narrow, narrow)
    lax.fori_loop(1, n_ex, start_narrow, 0)
    got_b[rows_of(ex), :] = send_b[rows_of(ex), :]

    def send_wide(shard, chunk, rows):
        def store_wide(c, value):
            send_a[shard, chunk, :, tile(c)] = value

        def start_wide(i, carry):
            a_copy(shard, chunk, lax.rem(ex + i, n_ex)).start()
            return carry

        scale(shard, rows, store_wide, part)
        lax.fori_loop(1, n_ex, start_wide, 0)
        got_a[shard, chunk, rows_of(ex), :] = send_a[shard, chunk, rows_of(ex), :]

    for chunk in range(CHUNKS):
        send_wide(hid, chunk, lambda c: cot[:, tile(c, chunk * part)])

    for i in range(1, n_hid):
        source = lax.rem(hid + i, n_hid)
        pltpu.make_async_copy(meta.at[source], meta.at[source], meta_recv.at[source]).wait()
    cnt[...] = jnp.zeros(cnt.shape, cnt.dtype)
    for shard in range(n_hid):
        live = jnp.where((meta[shard] >= 0.0) & (lane < n_ex), 1.0, 0.0)
        cnt[shard : shard + 1, :] = jnp.sum(live, axis=0, keepdims=True)

    def cnt_copy(i):
        return pltpu.make_async_remote_copy(
            src_ref=cnt, dst_ref=cnts.at[ex], send_sem=cnt_send, recv_sem=cnt_recv,
            device_id={"expert": lax.rem(ex + i, n_ex)}, device_id_type=MESH,
        )

    def send_cnt(i, carry):
        cnt_copy(i).start()
        return carry

    lax.fori_loop(1, n_ex, send_cnt, 0)
    cnts[ex] = cnt[...]
    pltpu.make_async_copy(cnts.at[pl.ds(0, n_ex - 1)], cnts.at[pl.ds(0, n_ex - 1)], cnt_recv).wait()

    one_lane = lax.broadcasted_iota(jnp.int32, (1, lanes), 1)

    def order(shard):
        number = lax.broadcasted_iota(jnp.int32, (1, n_ex * slots), 1).astype(jnp.float32)
        owner = jnp.floor((number + 0.5) / slots)
        place = number - owner * slots

        def add(source, carry):
            first, own = carry
            row = cnts[source, pl.ds(shard, 1), :]
            count = jnp.sum(jnp.where(one_lane == ex, row, 0.0), axis=1, keepdims=True)
            at = source.astype(jnp.float32)
            return first + jnp.where(owner > at, count, 0.0), own + jnp.where(owner == at, count, 0.0)

        zero = jnp.zeros(owner.shape, jnp.float32)
        first, own = lax.fori_loop(0, n_ex, add, (zero, zero))
        target = jnp.where(place < own, first + place, -1.0)
        row = lax.broadcasted_iota(jnp.int32, (group, owner.shape[1]), 0).astype(jnp.float32)
        put[shard] = jnp.where(row == target, 1.0, 0.0).astype(jnp.bfloat16)

    order(hid)

    pltpu.make_async_copy(got_b.at[pl.ds(0, peers_rows)], got_b.at[pl.ds(0, peers_rows)], b_recv).wait()
    routed_b[hid] = jnp.dot(put[hid], got_b[...], preferred_element_type=jnp.float32).astype(jnp.bfloat16)

    def start_routed(way):
        @pl.when(has_next(way))
        def _():
            routed_copy(way, hid).start()

    def on_line(step, body):
        def one(way):
            shard = hid - step + 2 * step * way

            @pl.when((shard >= 0) & (shard < n_hid))
            def _():
                body(way, shard)

        both_ways(one)

    def take_raw(way, shard, chunk):
        pltpu.make_async_copy(raw.at[shard, chunk], raw.at[shard, chunk], raw_recv.at[shard, chunk]).wait()

        @pl.when(has_next(way))
        def _():
            raw_copy(way, shard, chunk).start()

        send_wide(shard, chunk, lambda c: raw[shard, chunk, :, tile(c)])

    def take_routed(way, shard):
        pltpu.make_async_copy(routed_b.at[shard], routed_b.at[shard], rb_recv.at[shard]).wait()

        @pl.when(has_next(way))
        def _():
            routed_copy(way, shard).start()

    def along(step, carry):
        for chunk in range(CHUNKS):
            on_line(step, functools.partial(take_raw, chunk=chunk))
        last_raw(step)
        return carry

    def last_raw(step):
        def one(way):
            @pl.when(step == hid + way * (n_hid - 1 - 2 * hid))
            def _():
                start_routed(way)

        both_ways(one)

    last_raw(0)

    def order_other(i, carry):
        shard = lax.rem(hid + i, n_hid)
        choose(shard)
        order(shard)
        return carry

    lax.fori_loop(1, n_hid, order_other, 0)
    for c in range(w_tiles):
        weight_load(c).wait()
        weight_t[:, c * TILE : (c + 1) * TILE] = weight[c % 2].T
        if c + 2 < w_tiles:
            weight_load(c + 2).start()

    lax.fori_loop(1, n_hid, along, 0)

    def product(lhs, row, columns):
        return jnp.dot(lhs, weight_t[row : row + lhs.shape[1], columns], preferred_element_type=jnp.float32)

    def compact(shard, chunk):
        if n_ex > 1:
            arrived = got_a.at[shard, chunk, pl.ds(0, peers_rows)]
            pltpu.make_async_copy(arrived, arrived, a_recv.at[shard, chunk]).wait()

        def one(c, carry):
            rows = jnp.dot(put[shard], got_a[shard, chunk, :, tile(c)], preferred_element_type=jnp.float32)
            routed_a[:, tile(c)] = rows.astype(jnp.bfloat16)
            return carry

        lax.fori_loop(0, part // TILE, one, 0)

    def over_columns(body):
        def one(c, carry):
            body(tile(c))
            return carry

        lax.fori_loop(0, stage.shape[2] // TILE, one, 0)

    def finish(way, shard, early):
        for chunk in range(CHUNKS - 1):
            compact(shard, chunk)

            def add(columns, chunk=chunk):
                value = product(routed_a[...], chunk * part, columns)
                total[:, columns] = value if chunk == 0 else total[:, columns] + value

            over_columns(add)

        @pl.when(jnp.logical_not(early))
        def _():
            take_routed(way, shard)

        def add_routed(columns):
            total[:, columns] = total[:, columns] + product(routed_b[shard], wide, columns)

        over_columns(add_routed)
        compact(shard, CHUNKS - 1)
        rows = pl.ds(pl.multiple_of(shard * group, 16), group)

        def write(columns):
            value = total[:, columns] + product(routed_a[...], (CHUNKS - 1) * part, columns)
            stage[0, rows, columns] = value.astype(jnp.bfloat16)

        over_columns(write)

    def take_to_pass(way, shard):
        @pl.when(has_next(way))
        def _():
            take_routed(way, shard)

    def along_routed(step, carry):
        @pl.when(step > 0)
        def _():
            on_line(step, take_to_pass)

        def one(way, inner):
            shard = hid - step + 2 * step * way

            @pl.when((shard >= 0) & (shard < n_hid))
            def _():
                finish(way, shard, (step == 0) | has_next(way))

            return inner

        lax.fori_loop(0, jnp.where(step > 0, 2, 1), one, 0)
        return carry

    lax.fori_loop(0, n_hid, along_routed, 0)

    for shard in range(n_hid):
        for chunk in range(CHUNKS):
            sent_rows = send_a.at[shard, chunk, pl.ds(0, peers_rows)]
            pltpu.make_async_copy(sent_rows, sent_rows, a_send.at[shard, chunk]).wait()
        for way in range(2):
            sent = has_next(way) & ((shard <= hid) if way == 0 else (shard >= hid))

            @pl.when(sent)
            def _():
                for chunk in range(CHUNKS):
                    raw_copy(way, shard, chunk).wait_send()
                routed_copy(way, shard).wait_send()

    sent_rows = send_b.at[pl.ds(0, peers_rows)]
    pltpu.make_async_copy(sent_rows, sent_rows, b_send).wait()
    pltpu.make_async_copy(cnts.at[pl.ds(0, n_ex - 1)], cnts.at[pl.ds(0, n_ex - 1)], cnt_send).wait()
    for i in range(1, n_hid):
        meta_copy(i).wait_send()


def shards(n_ex, n_hid, cotangent, slot_token, slot_gate, w_down):
    tokens, features = cotangent.shape
    hidden = w_down.shape[1]
    slots = -(-slot_token.shape[2] // 16) * 16
    lanes = -(-2 * n_ex // 128) * 128
    wide = features * 3 // 4 // (CHUNKS * TILE) * CHUNKS * TILE
    part = wide // CHUNKS
    narrow = features - wide
    group = CF * tokens
    dma = pltpu.SemaphoreType.DMA
    bf16, f32 = jnp.bfloat16, jnp.float32
    hbm = pl.BlockSpec(memory_space=pltpu.HBM)
    return pl.pallas_call(
        functools.partial(kernel, n_ex, n_hid, slots),
        out_shape=pltpu.VMEM((1, n_hid * group, hidden), bf16),
        in_specs=[hbm, hbm, hbm, hbm],
        out_specs=pl.BlockSpec(memory_space=pltpu.VMEM),
        scratch_shapes=[
            pltpu.VMEM(cotangent.shape, bf16),
            pltpu.VMEM(slot_token.shape, jnp.int32),
            pltpu.VMEM(slot_gate.shape, f32),
            pltpu.VMEM((n_hid, n_ex * slots, tokens), bf16),
            pltpu.VMEM((n_hid, n_ex * slots, 128), f32),
            pltpu.VMEM((n_hid, group, n_ex * slots), bf16),
            pltpu.VMEM((features, hidden), bf16),
            pltpu.VMEM((group, hidden), f32),
            pltpu.VMEM((n_hid, CHUNKS, tokens, part), bf16),
            pltpu.VMEM((lanes, 128), f32),
            pltpu.VMEM((n_hid, slots, lanes), f32),
            pltpu.VMEM((-(-n_hid // 8) * 8, lanes), f32),
            pltpu.VMEM((n_ex, -(-n_hid // 8) * 8, lanes), f32),
            pltpu.VMEM((n_hid, CHUNKS, n_ex * slots, part), bf16),
            pltpu.VMEM((n_ex * slots, narrow), bf16),
            pltpu.VMEM((n_hid, CHUNKS, n_ex * slots, part), bf16),
            pltpu.VMEM((n_ex * slots, narrow), bf16),
            pltpu.VMEM((n_hid, group, narrow), bf16),
            pltpu.VMEM((group, part), bf16),
            pltpu.VMEM((2, TILE, features), bf16),
            dma((2, n_hid, CHUNKS)), dma((n_hid, CHUNKS)), dma((n_hid,)), dma((n_hid,)), dma, dma,
            dma((n_hid, CHUNKS)), dma((n_hid, CHUNKS)), dma, dma, dma((2, n_hid)), dma((n_hid,)), dma((5,)),
        ],
        compiler_params=pltpu.CompilerParams(
            collective_id=0, has_side_effects=True, vmem_limit_bytes=56 * 1024 * 1024
        ),
        cost_estimate=pl.CostEstimate(
            flops=2 * n_hid * group * hidden * features, bytes_accessed=2 * hidden * features * 3, transcendentals=0
        ),
        name="route_and_multiply",
    )(cotangent, slot_token, slot_gate, w_down)


def solution(mesh):
    n_ex, n_hid = mesh.shape["expert"], mesh.shape["hidden"]
    in_specs = (
        P(("expert", "hidden"), None),
        P(("expert", "hidden"), None, None),
        P(("expert", "hidden"), None, None),
        P("expert", "hidden", None),
    )
    out_specs = P("expert", None, "hidden")
    return jax.shard_map(
        functools.partial(shards, n_ex, n_hid), mesh=mesh, in_specs=in_specs, out_specs=out_specs, check_vma=False
    )
```

```python
import functools

import jax
import jax.numpy as jnp
from jax import lax
from jax.experimental import pallas as pl
from jax.experimental.pallas import tpu as pltpu
from jax.sharding import PartitionSpec as P

CF = 2
CHUNKS = 2
RAW_SHARE = 11, 16
TILE = 256
MESH = pl.DeviceIdType.MESH


def tile_of(width):
    return width if width <= 640 else TILE if width % TILE == 0 else 128


def kernel(
    n_ex, n_hid, slots, widths, cot_hbm, token_hbm, gate_hbm, w_hbm, stage,
    cot, token_in, gate_in, pick, gates, put, weight_t, total,
    raw, table, meta, cnt, cnts, send_a, send_b, got_a, got_b, routed_b, routed_a, weight,
    raw_send, raw_recv, meta_send, meta_recv, cnt_send, cnt_recv,
    a_send, a_recv, b_send, b_recv, rb_send, rb_recv, load_sem,
):
    ex, hid = lax.axis_index("expert"), lax.axis_index("hidden")
    tokens = cot.shape[0]
    starts = [sum(widths[:chunk]) for chunk in range(CHUNKS)]
    wide = sum(widths)
    narrow = send_b.shape[1]
    group = routed_b.shape[1]
    lanes = meta.shape[2]
    peers_rows = (n_ex - 1) * slots

    def rows_of(i):
        return pl.ds(pl.multiple_of(i * slots, 16), slots)

    loads = [
        pltpu.make_async_copy(source, target, load_sem.at[i])
        for i, (source, target) in enumerate(
            [(token_hbm, token_in), (gate_hbm, gate_in), (cot_hbm, cot)]
        )
    ]
    for load in loads:
        load.start()

    def weight_load(c):
        rows = pl.ds(c * TILE, TILE)
        return pltpu.make_async_copy(w_hbm.at[0, rows], weight.at[c % 2], load_sem.at[3 + c % 2])

    w_tiles = w_hbm.shape[1] // TILE
    for c in range(min(2, w_tiles)):
        weight_load(c).start()

    barrier = pltpu.get_barrier_semaphore()

    def greet_plane(i, carry):
        pl.semaphore_signal(barrier, inc=1, device_id={"expert": lax.rem(ex + i, n_ex)}, device_id_type=MESH)
        return carry

    def greet_line(i, carry):
        pl.semaphore_signal(barrier, inc=1, device_id={"hidden": lax.rem(hid + i, n_hid)}, device_id_type=MESH)
        return carry

    lax.fori_loop(1, n_ex, greet_plane, 0)
    lax.fori_loop(1, n_hid, greet_line, 0)
    pl.semaphore_wait(barrier, n_ex + n_hid - 2)

    def meta_copy(i):
        return pltpu.make_async_remote_copy(
            src_ref=meta.at[hid], dst_ref=meta.at[hid], send_sem=meta_send.at[i], recv_sem=meta_recv.at[hid],
            device_id={"hidden": lax.rem(hid + i, n_hid)}, device_id_type=MESH,
        )

    def to_next(src, dst, send, recv, way):
        return pltpu.make_async_remote_copy(
            src_ref=src, dst_ref=dst, send_sem=send, recv_sem=recv,
            device_id={"hidden": hid + 1 - 2 * way}, device_id_type=MESH,
        )

    def raw_copy(way, shard, chunk, own=False):
        held = raw.at[shard, chunk, :, pl.ds(0, widths[chunk])]
        src = cot_hbm.at[:, pl.ds(starts[chunk], widths[chunk])] if own else held
        return to_next(src, held, raw_send.at[way, shard, chunk], raw_recv.at[shard, chunk], way)

    def routed_copy(way, shard):
        held = routed_b.at[shard]
        return to_next(held, held, rb_send.at[way, shard], rb_recv.at[shard], way)

    def has_next(way):
        after = hid + 1 - 2 * way
        return (after >= 0) & (after < n_hid)

    def both_ways(body):
        def step(way, carry):
            body(way)
            return carry

        lax.fori_loop(0, 2, step, 0)

    def start_raw(way, chunk):
        @pl.when(has_next(way))
        def _():
            raw_copy(way, hid, chunk, own=True).start()

    for chunk in range(CHUNKS):
        both_ways(functools.partial(start_raw, chunk=chunk))
    loads[0].wait()
    loads[1].wait()
    live_slots = token_in.shape[2]
    table[...] = jnp.where(lax.broadcasted_iota(jnp.int32, table.shape, 0) < n_ex, -1.0, 0.0)
    table[0:n_ex, 0:live_slots] = token_in[0].astype(jnp.float32)
    table[n_ex : 2 * n_ex, 0:live_slots] = gate_in[0]
    meta[hid] = table[...].T[0:slots, :]
    for i in range(1, n_hid):
        meta_copy(i).start()

    lane = lax.broadcasted_iota(jnp.int32, (slots, lanes), 1)
    token_iota = lax.broadcasted_iota(jnp.int32, (slots, tokens), 1).astype(jnp.float32)

    def choose(shard):
        held = meta[shard]

        def one(expert, carry):
            token = jnp.sum(jnp.where(lane == expert, held, 0.0), axis=1, keepdims=True)
            gate = jnp.sum(jnp.where(lane == expert + n_ex, held, 0.0), axis=1, keepdims=True)
            pick[shard, rows_of(expert), :] = jnp.where(token == token_iota, 1.0, 0.0).astype(jnp.bfloat16)
            gates[shard, rows_of(expert), :] = jnp.broadcast_to(gate, (slots, 128))
            return carry

        lax.fori_loop(0, n_ex, one, 0)

    def tile(c, base=0, size=TILE):
        return pl.ds(pl.multiple_of(base + c * size, 128), size)

    def scale(shard, rows, store, columns):
        size = tile_of(columns)

        def one(c, carry):
            rows_c = jnp.dot(pick[shard], rows(c, size), preferred_element_type=jnp.float32)
            gate = jnp.concatenate([gates[shard]] * (size // 128), axis=1)
            store(c, size, (gate * rows_c).astype(jnp.bfloat16))
            return carry

        lax.fori_loop(0, columns // size, one, 0)

    def a_copy(shard, chunk, expert):
        return pltpu.make_async_remote_copy(
            src_ref=send_a.at[shard, chunk, rows_of(expert), pl.ds(0, widths[chunk])],
            dst_ref=got_a.at[shard, chunk, rows_of(ex), pl.ds(0, widths[chunk])],
            send_sem=a_send.at[shard, chunk], recv_sem=a_recv.at[shard, chunk],
            device_id={"expert": expert}, device_id_type=MESH,
        )

    def b_copy(expert):
        return pltpu.make_async_remote_copy(
            src_ref=send_b.at[rows_of(expert)], dst_ref=got_b.at[rows_of(ex)],
            send_sem=b_send, recv_sem=b_recv, device_id={"expert": expert}, device_id_type=MESH,
        )

    def store_narrow(c, size, value):
        send_b[:, tile(c, 0, size)] = value

    def start_narrow(i, carry):
        b_copy(lax.rem(ex + i, n_ex)).start()
        return carry

    choose(hid)
    loads[2].wait()
    scale(hid, lambda c, size: cot[:, tile(c, wide, size)], store_narrow, narrow)
    lax.fori_loop(1, n_ex, start_narrow, 0)
    got_b[rows_of(ex), :] = send_b[rows_of(ex), :]

    def send_wide(shard, chunk, rows):
        def store_wide(c, size, value):
            send_a[shard, chunk, :, tile(c, 0, size)] = value

        def start_wide(i, carry):
            a_copy(shard, chunk, lax.rem(ex + i, n_ex)).start()
            return carry

        scale(shard, rows, store_wide, widths[chunk])
        lax.fori_loop(1, n_ex, start_wide, 0)
        own = slice(0, widths[chunk])
        got_a[shard, chunk, rows_of(ex), own] = send_a[shard, chunk, rows_of(ex), own]

    for chunk in range(CHUNKS):
        send_wide(hid, chunk, lambda c, size: cot[:, tile(c, starts[chunk], size)])

    for i in range(1, n_hid):
        source = lax.rem(hid + i, n_hid)
        pltpu.make_async_copy(meta.at[source], meta.at[source], meta_recv.at[source]).wait()
    cnt[...] = jnp.zeros(cnt.shape, cnt.dtype)
    for shard in range(n_hid):
        live = jnp.where((meta[shard] >= 0.0) & (lane < n_ex), 1.0, 0.0)
        cnt[shard : shard + 1, :] = jnp.sum(live, axis=0, keepdims=True)

    def cnt_copy(i):
        return pltpu.make_async_remote_copy(
            src_ref=cnt, dst_ref=cnts.at[ex], send_sem=cnt_send, recv_sem=cnt_recv,
            device_id={"expert": lax.rem(ex + i, n_ex)}, device_id_type=MESH,
        )

    def send_cnt(i, carry):
        cnt_copy(i).start()
        return carry

    lax.fori_loop(1, n_ex, send_cnt, 0)
    cnts[ex] = cnt[...]
    pltpu.make_async_copy(cnts.at[pl.ds(0, n_ex - 1)], cnts.at[pl.ds(0, n_ex - 1)], cnt_recv).wait()

    one_lane = lax.broadcasted_iota(jnp.int32, (1, lanes), 1)

    def order(shard):
        number = lax.broadcasted_iota(jnp.int32, (1, n_ex * slots), 1).astype(jnp.float32)
        owner = jnp.floor((number + 0.5) / slots)
        place = number - owner * slots

        def add(source, carry):
            first, own = carry
            row = cnts[source, pl.ds(shard, 1), :]
            count = jnp.sum(jnp.where(one_lane == ex, row, 0.0), axis=1, keepdims=True)
            at = source.astype(jnp.float32)
            return first + jnp.where(owner > at, count, 0.0), own + jnp.where(owner == at, count, 0.0)

        zero = jnp.zeros(owner.shape, jnp.float32)
        first, own = lax.fori_loop(0, n_ex, add, (zero, zero))
        target = jnp.where(place < own, first + place, -1.0)
        row = lax.broadcasted_iota(jnp.int32, (group, owner.shape[1]), 0).astype(jnp.float32)
        put[shard] = jnp.where(row == target, 1.0, 0.0).astype(jnp.bfloat16)

    order(hid)

    pltpu.make_async_copy(got_b.at[pl.ds(0, peers_rows)], got_b.at[pl.ds(0, peers_rows)], b_recv).wait()
    routed_b[hid] = jnp.dot(put[hid], got_b[...], preferred_element_type=jnp.float32).astype(jnp.bfloat16)

    def start_routed(way):
        @pl.when(has_next(way))
        def _():
            routed_copy(way, hid).start()

    def on_line(step, body):
        def one(way):
            shard = hid - step + 2 * step * way

            @pl.when((shard >= 0) & (shard < n_hid))
            def _():
                body(way, shard)

        both_ways(one)

    def take_raw(way, shard, chunk):
        held = raw.at[shard, chunk, :, pl.ds(0, widths[chunk])]
        pltpu.make_async_copy(held, held, raw_recv.at[shard, chunk]).wait()

        @pl.when(has_next(way))
        def _():
            raw_copy(way, shard, chunk).start()

        send_wide(shard, chunk, lambda c, size: raw[shard, chunk, :, tile(c, 0, size)])

    def take_routed(way, shard):
        pltpu.make_async_copy(routed_b.at[shard], routed_b.at[shard], rb_recv.at[shard]).wait()

        @pl.when(has_next(way))
        def _():
            routed_copy(way, shard).start()

    def along(step, carry):
        for chunk in range(CHUNKS):
            on_line(step, functools.partial(take_raw, chunk=chunk))
        last_raw(step)
        return carry

    def last_raw(step):
        def one(way):
            @pl.when(step == hid + way * (n_hid - 1 - 2 * hid))
            def _():
                start_routed(way)

        both_ways(one)

    last_raw(0)

    def order_other(i, carry):
        shard = lax.rem(hid + i, n_hid)
        choose(shard)
        order(shard)
        return carry

    lax.fori_loop(1, n_hid, order_other, 0)
    for c in range(w_tiles):
        weight_load(c).wait()
        weight_t[:, c * TILE : (c + 1) * TILE] = weight[c % 2].T
        if c + 2 < w_tiles:
            weight_load(c + 2).start()

    lax.fori_loop(1, n_hid, along, 0)

    def product(lhs, row, columns):
        return jnp.dot(lhs, weight_t[row : row + lhs.shape[1], columns], preferred_element_type=jnp.float32)

    def compact(shard, chunk):
        if n_ex > 1:
            arrived = got_a.at[shard, chunk, pl.ds(0, peers_rows), pl.ds(0, widths[chunk])]
            pltpu.make_async_copy(arrived, arrived, a_recv.at[shard, chunk]).wait()

        def one(c, carry):
            columns = tile(c, 0, size)
            rows = jnp.dot(put[shard], got_a[shard, chunk, :, columns], preferred_element_type=jnp.float32)
            routed_a[:, columns] = rows.astype(jnp.bfloat16)
            return carry

        size = tile_of(widths[chunk])
        lax.fori_loop(0, widths[chunk] // size, one, 0)

    def over_columns(body):
        def one(c, carry):
            body(tile(c))
            return carry

        lax.fori_loop(0, stage.shape[2] // TILE, one, 0)

    def finish(way, shard, early):
        for chunk in range(CHUNKS - 1):
            compact(shard, chunk)

            def add(columns, chunk=chunk):
                value = product(routed_a[:, : widths[chunk]], starts[chunk], columns)
                total[:, columns] = value if chunk == 0 else total[:, columns] + value

            over_columns(add)

        @pl.when(jnp.logical_not(early))
        def _():
            take_routed(way, shard)

        def add_routed(columns):
            total[:, columns] = total[:, columns] + product(routed_b[shard], wide, columns)

        over_columns(add_routed)
        compact(shard, CHUNKS - 1)
        rows = pl.ds(pl.multiple_of(shard * group, 16), group)

        def write(columns):
            value = total[:, columns] + product(routed_a[:, : widths[-1]], starts[-1], columns)
            stage[0, rows, columns] = value.astype(jnp.bfloat16)

        over_columns(write)

    def take_to_pass(way, shard):
        @pl.when(has_next(way))
        def _():
            take_routed(way, shard)

    def along_routed(step, carry):
        @pl.when(step > 0)
        def _():
            on_line(step, take_to_pass)

        def one(way, inner):
            shard = hid - step + 2 * step * way

            @pl.when((shard >= 0) & (shard < n_hid))
            def _():
                finish(way, shard, (step == 0) | has_next(way))

            return inner

        lax.fori_loop(0, jnp.where(step > 0, 2, 1), one, 0)
        return carry

    lax.fori_loop(0, n_hid, along_routed, 0)

    for shard in range(n_hid):
        for chunk in range(CHUNKS):
            sent_rows = send_a.at[shard, chunk, pl.ds(0, peers_rows), pl.ds(0, widths[chunk])]
            pltpu.make_async_copy(sent_rows, sent_rows, a_send.at[shard, chunk]).wait()
        for way in range(2):
            sent = has_next(way) & ((shard <= hid) if way == 0 else (shard >= hid))

            @pl.when(sent)
            def _():
                for chunk in range(CHUNKS):
                    raw_copy(way, shard, chunk).wait_send()
                routed_copy(way, shard).wait_send()

    sent_rows = send_b.at[pl.ds(0, peers_rows)]
    pltpu.make_async_copy(sent_rows, sent_rows, b_send).wait()
    pltpu.make_async_copy(cnts.at[pl.ds(0, n_ex - 1)], cnts.at[pl.ds(0, n_ex - 1)], cnt_send).wait()
    for i in range(1, n_hid):
        meta_copy(i).wait_send()


def shards(n_ex, n_hid, cotangent, slot_token, slot_gate, w_down):
    tokens, features = cotangent.shape
    hidden = w_down.shape[1]
    slots = -(-slot_token.shape[2] // 16) * 16
    lanes = -(-2 * n_ex // 128) * 128
    wide = features * RAW_SHARE[0] // RAW_SHARE[1] // 128 * 128
    part = -(-wide // (128 * CHUNKS)) * 128
    widths = tuple(min(part, wide - chunk * part) for chunk in range(CHUNKS))
    narrow = features - wide
    group = CF * tokens
    dma = pltpu.SemaphoreType.DMA
    bf16, f32 = jnp.bfloat16, jnp.float32
    hbm = pl.BlockSpec(memory_space=pltpu.HBM)
    return pl.pallas_call(
        functools.partial(kernel, n_ex, n_hid, slots, widths),
        out_shape=pltpu.VMEM((1, n_hid * group, hidden), bf16),
        in_specs=[hbm, hbm, hbm, hbm],
        out_specs=pl.BlockSpec(memory_space=pltpu.VMEM),
        scratch_shapes=[
            pltpu.VMEM(cotangent.shape, bf16),
            pltpu.VMEM(slot_token.shape, jnp.int32),
            pltpu.VMEM(slot_gate.shape, f32),
            pltpu.VMEM((n_hid, n_ex * slots, tokens), bf16),
            pltpu.VMEM((n_hid, n_ex * slots, 128), f32),
            pltpu.VMEM((n_hid, group, n_ex * slots), bf16),
            pltpu.VMEM((features, hidden), bf16),
            pltpu.VMEM((group, hidden), f32),
            pltpu.VMEM((n_hid, CHUNKS, tokens, part), bf16),
            pltpu.VMEM((lanes, 128), f32),
            pltpu.VMEM((n_hid, slots, lanes), f32),
            pltpu.VMEM((-(-n_hid // 8) * 8, lanes), f32),
            pltpu.VMEM((n_ex, -(-n_hid // 8) * 8, lanes), f32),
            pltpu.VMEM((n_hid, CHUNKS, n_ex * slots, part), bf16),
            pltpu.VMEM((n_ex * slots, narrow), bf16),
            pltpu.VMEM((n_hid, CHUNKS, n_ex * slots, part), bf16),
            pltpu.VMEM((n_ex * slots, narrow), bf16),
            pltpu.VMEM((n_hid, group, narrow), bf16),
            pltpu.VMEM((group, part), bf16),
            pltpu.VMEM((2, TILE, features), bf16),
            dma((2, n_hid, CHUNKS)), dma((n_hid, CHUNKS)), dma((n_hid,)), dma((n_hid,)), dma, dma,
            dma((n_hid, CHUNKS)), dma((n_hid, CHUNKS)), dma, dma, dma((2, n_hid)), dma((n_hid,)), dma((5,)),
        ],
        compiler_params=pltpu.CompilerParams(
            collective_id=0, has_side_effects=True, vmem_limit_bytes=56 * 1024 * 1024
        ),
        cost_estimate=pl.CostEstimate(
            flops=2 * n_hid * group * hidden * features, bytes_accessed=2 * hidden * features * 3, transcendentals=0
        ),
        name="route_and_multiply",
    )(cotangent, slot_token, slot_gate, w_down)


def solution(mesh):
    n_ex, n_hid = mesh.shape["expert"], mesh.shape["hidden"]
    in_specs = (
        P(("expert", "hidden"), None),
        P(("expert", "hidden"), None, None),
        P(("expert", "hidden"), None, None),
        P("expert", "hidden", None),
    )
    out_specs = P("expert", None, "hidden")
    return jax.shard_map(
        functools.partial(shards, n_ex, n_hid), mesh=mesh, in_specs=in_specs, out_specs=out_specs, check_vma=False
    )
```

```python
import functools

import jax
import jax.numpy as jnp
from jax import lax
from jax.experimental import pallas as pl
from jax.experimental.pallas import tpu as pltpu
from jax.sharding import PartitionSpec as P

CF = 2
CHUNKS = 2
RAW_SHARE = 13, 16
TILE = 256
MESH = pl.DeviceIdType.MESH


def tile_of(width):
    return width if width <= 640 else TILE if width % TILE == 0 else 128


def kernel(
    n_ex, n_hid, slots, widths, cot_hbm, token_hbm, gate_hbm, w_hbm, stage,
    cot, token_in, gate_in, pick, gates, put, weight_t, total,
    raw, table, meta, cnt, cnts, send_a, send_b, got_a, got_b, routed_b, routed_a, weight,
    raw_send, raw_recv, meta_send, meta_recv, cnt_send, cnt_recv,
    a_send, a_recv, b_send, b_recv, rb_send, rb_recv, load_sem,
):
    ex, hid = lax.axis_index("expert"), lax.axis_index("hidden")
    tokens = cot.shape[0]
    def span(chunk):
        return pl.ds(starts[chunk], widths[chunk])

    starts = [sum(widths[:chunk]) for chunk in range(CHUNKS)]
    wide = sum(widths)
    narrow = send_b.shape[1]
    group = routed_b.shape[1]
    lanes = meta.shape[2]
    peers_rows = (n_ex - 1) * slots

    def rows_of(i):
        return pl.ds(pl.multiple_of(i * slots, 16), slots)

    loads = [
        pltpu.make_async_copy(source, target, load_sem.at[i])
        for i, (source, target) in enumerate(
            [(token_hbm, token_in), (gate_hbm, gate_in), (cot_hbm, cot)]
        )
    ]
    for load in loads:
        load.start()

    def weight_load(c):
        rows = pl.ds(c * TILE, TILE)
        return pltpu.make_async_copy(w_hbm.at[0, rows], weight.at[c % 2], load_sem.at[3 + c % 2])

    w_tiles = w_hbm.shape[1] // TILE
    for c in range(min(2, w_tiles)):
        weight_load(c).start()

    barrier = pltpu.get_barrier_semaphore()

    def greet_plane(i, carry):
        pl.semaphore_signal(barrier, inc=1, device_id={"expert": lax.rem(ex + i, n_ex)}, device_id_type=MESH)
        return carry

    def greet_line(i, carry):
        pl.semaphore_signal(barrier, inc=1, device_id={"hidden": lax.rem(hid + i, n_hid)}, device_id_type=MESH)
        return carry

    lax.fori_loop(1, n_ex, greet_plane, 0)
    lax.fori_loop(1, n_hid, greet_line, 0)
    pl.semaphore_wait(barrier, n_ex + n_hid - 2)

    def meta_copy(i):
        return pltpu.make_async_remote_copy(
            src_ref=meta.at[hid], dst_ref=meta.at[hid], send_sem=meta_send.at[i], recv_sem=meta_recv.at[hid],
            device_id={"hidden": lax.rem(hid + i, n_hid)}, device_id_type=MESH,
        )

    def to_next(src, dst, send, recv, way):
        return pltpu.make_async_remote_copy(
            src_ref=src, dst_ref=dst, send_sem=send, recv_sem=recv,
            device_id={"hidden": hid + 1 - 2 * way}, device_id_type=MESH,
        )

    def raw_copy(way, shard, chunk, own=False):
        held = raw.at[shard, :, span(chunk)]
        src = cot_hbm.at[:, pl.ds(starts[chunk], widths[chunk])] if own else held
        return to_next(src, held, raw_send.at[way, shard, chunk], raw_recv.at[shard, chunk], way)

    def routed_copy(way, shard):
        held = routed_b.at[shard]
        return to_next(held, held, rb_send.at[way, shard], rb_recv.at[shard], way)

    def has_next(way):
        after = hid + 1 - 2 * way
        return (after >= 0) & (after < n_hid)

    def both_ways(body):
        def step(way, carry):
            body(way)
            return carry

        lax.fori_loop(0, 2, step, 0)

    def start_raw(way, chunk):
        @pl.when(has_next(way))
        def _():
            raw_copy(way, hid, chunk, own=True).start()

    for chunk in range(CHUNKS):
        both_ways(functools.partial(start_raw, chunk=chunk))
    loads[0].wait()
    loads[1].wait()
    live_slots = token_in.shape[2]
    table[...] = jnp.where(lax.broadcasted_iota(jnp.int32, table.shape, 0) < n_ex, -1.0, 0.0)
    table[0:n_ex, 0:live_slots] = token_in[0].astype(jnp.float32)
    table[n_ex : 2 * n_ex, 0:live_slots] = gate_in[0]
    meta[hid] = table[...].T[0:slots, :]
    for i in range(1, n_hid):
        meta_copy(i).start()

    lane = lax.broadcasted_iota(jnp.int32, (slots, lanes), 1)
    token_iota = lax.broadcasted_iota(jnp.int32, (slots, tokens), 1).astype(jnp.float32)

    def choose(shard):
        held = meta[shard]

        def one(expert, carry):
            token = jnp.sum(jnp.where(lane == expert, held, 0.0), axis=1, keepdims=True)
            gate = jnp.sum(jnp.where(lane == expert + n_ex, held, 0.0), axis=1, keepdims=True)
            pick[shard, rows_of(expert), :] = jnp.where(token == token_iota, 1.0, 0.0).astype(jnp.bfloat16)
            gates[shard, rows_of(expert), :] = jnp.broadcast_to(gate, (slots, 128))
            return carry

        lax.fori_loop(0, n_ex, one, 0)

    def tile(c, base=0, size=TILE):
        return pl.ds(pl.multiple_of(base + c * size, 128), size)

    def scale(shard, rows, store, columns):
        size = tile_of(columns)

        def one(c, carry):
            rows_c = jnp.dot(pick[shard], rows(c, size), preferred_element_type=jnp.float32)
            gate = jnp.concatenate([gates[shard]] * (size // 128), axis=1)
            store(c, size, (gate * rows_c).astype(jnp.bfloat16))
            return carry

        lax.fori_loop(0, columns // size, one, 0)

    def a_copy(shard, chunk, expert):
        return pltpu.make_async_remote_copy(
            src_ref=send_a.at[shard, rows_of(expert), span(chunk)],
            dst_ref=got_a.at[shard, rows_of(ex), span(chunk)],
            send_sem=a_send.at[shard, chunk], recv_sem=a_recv.at[shard, chunk],
            device_id={"expert": expert}, device_id_type=MESH,
        )

    def b_copy(expert):
        return pltpu.make_async_remote_copy(
            src_ref=send_b.at[rows_of(expert)], dst_ref=got_b.at[rows_of(ex)],
            send_sem=b_send, recv_sem=b_recv, device_id={"expert": expert}, device_id_type=MESH,
        )

    def store_narrow(c, size, value):
        send_b[:, tile(c, 0, size)] = value

    def start_narrow(i, carry):
        b_copy(lax.rem(ex + i, n_ex)).start()
        return carry

    choose(hid)
    loads[2].wait()
    scale(hid, lambda c, size: cot[:, tile(c, wide, size)], store_narrow, narrow)
    lax.fori_loop(1, n_ex, start_narrow, 0)
    got_b[rows_of(ex), :] = send_b[rows_of(ex), :]

    def send_wide(shard, chunk, rows):
        def store_wide(c, size, value):
            send_a[shard, :, tile(c, starts[chunk], size)] = value

        def start_wide(i, carry):
            a_copy(shard, chunk, lax.rem(ex + i, n_ex)).start()
            return carry

        scale(shard, rows, store_wide, widths[chunk])
        lax.fori_loop(1, n_ex, start_wide, 0)
        got_a[shard, rows_of(ex), span(chunk)] = send_a[shard, rows_of(ex), span(chunk)]

    for chunk in range(CHUNKS):
        send_wide(hid, chunk, lambda c, size: cot[:, tile(c, starts[chunk], size)])

    for i in range(1, n_hid):
        source = lax.rem(hid + i, n_hid)
        pltpu.make_async_copy(meta.at[source], meta.at[source], meta_recv.at[source]).wait()
    cnt[...] = jnp.zeros(cnt.shape, cnt.dtype)
    for shard in range(n_hid):
        live = jnp.where((meta[shard] >= 0.0) & (lane < n_ex), 1.0, 0.0)
        cnt[shard : shard + 1, :] = jnp.sum(live, axis=0, keepdims=True)

    def cnt_copy(i):
        return pltpu.make_async_remote_copy(
            src_ref=cnt, dst_ref=cnts.at[ex], send_sem=cnt_send, recv_sem=cnt_recv,
            device_id={"expert": lax.rem(ex + i, n_ex)}, device_id_type=MESH,
        )

    def send_cnt(i, carry):
        cnt_copy(i).start()
        return carry

    lax.fori_loop(1, n_ex, send_cnt, 0)
    cnts[ex] = cnt[...]
    pltpu.make_async_copy(cnts.at[pl.ds(0, n_ex - 1)], cnts.at[pl.ds(0, n_ex - 1)], cnt_recv).wait()

    one_lane = lax.broadcasted_iota(jnp.int32, (1, lanes), 1)

    def order(shard):
        number = lax.broadcasted_iota(jnp.int32, (1, n_ex * slots), 1).astype(jnp.float32)
        owner = jnp.floor((number + 0.5) / slots)
        place = number - owner * slots

        def add(source, carry):
            first, own = carry
            row = cnts[source, pl.ds(shard, 1), :]
            count = jnp.sum(jnp.where(one_lane == ex, row, 0.0), axis=1, keepdims=True)
            at = source.astype(jnp.float32)
            return first + jnp.where(owner > at, count, 0.0), own + jnp.where(owner == at, count, 0.0)

        zero = jnp.zeros(owner.shape, jnp.float32)
        first, own = lax.fori_loop(0, n_ex, add, (zero, zero))
        target = jnp.where(place < own, first + place, -1.0)
        row = lax.broadcasted_iota(jnp.int32, (group, owner.shape[1]), 0).astype(jnp.float32)
        put[shard] = jnp.where(row == target, 1.0, 0.0).astype(jnp.bfloat16)

    order(hid)

    pltpu.make_async_copy(got_b.at[pl.ds(0, peers_rows)], got_b.at[pl.ds(0, peers_rows)], b_recv).wait()
    routed_b[hid] = jnp.dot(put[hid], got_b[...], preferred_element_type=jnp.float32).astype(jnp.bfloat16)

    def start_routed(way):
        @pl.when(has_next(way))
        def _():
            routed_copy(way, hid).start()

    def on_line(step, body):
        def one(way):
            shard = hid - step + 2 * step * way

            @pl.when((shard >= 0) & (shard < n_hid))
            def _():
                body(way, shard)

        both_ways(one)

    def take_raw(way, shard, chunk):
        held = raw.at[shard, :, span(chunk)]
        pltpu.make_async_copy(held, held, raw_recv.at[shard, chunk]).wait()

        @pl.when(has_next(way))
        def _():
            raw_copy(way, shard, chunk).start()

        send_wide(shard, chunk, lambda c, size: raw[shard, :, tile(c, starts[chunk], size)])

    def take_routed(way, shard):
        pltpu.make_async_copy(routed_b.at[shard], routed_b.at[shard], rb_recv.at[shard]).wait()

        @pl.when(has_next(way))
        def _():
            routed_copy(way, shard).start()

    def along(step, carry):
        for chunk in range(CHUNKS):
            on_line(step, functools.partial(take_raw, chunk=chunk))
        last_raw(step)
        return carry

    def last_raw(step):
        def one(way):
            @pl.when(step == hid + way * (n_hid - 1 - 2 * hid))
            def _():
                start_routed(way)

        both_ways(one)

    last_raw(0)

    def order_other(i, carry):
        shard = lax.rem(hid + i, n_hid)
        choose(shard)
        order(shard)
        return carry

    lax.fori_loop(1, n_hid, order_other, 0)
    for c in range(w_tiles):
        weight_load(c).wait()
        weight_t[:, c * TILE : (c + 1) * TILE] = weight[c % 2].T
        if c + 2 < w_tiles:
            weight_load(c + 2).start()

    lax.fori_loop(1, n_hid, along, 0)

    def product(lhs, row, columns):
        return jnp.dot(lhs, weight_t[row : row + lhs.shape[1], columns], preferred_element_type=jnp.float32)

    def compact(shard, chunk):
        if n_ex > 1:
            arrived = got_a.at[shard, pl.ds(0, peers_rows), span(chunk)]
            pltpu.make_async_copy(arrived, arrived, a_recv.at[shard, chunk]).wait()

        def one(c, carry):
            columns = tile(c, 0, size)
            rows = jnp.dot(put[shard], got_a[shard, :, tile(c, starts[chunk], size)], preferred_element_type=jnp.float32)
            routed_a[:, columns] = rows.astype(jnp.bfloat16)
            return carry

        size = tile_of(widths[chunk])
        lax.fori_loop(0, widths[chunk] // size, one, 0)

    def over_columns(body):
        def one(c, carry):
            body(tile(c))
            return carry

        lax.fori_loop(0, stage.shape[2] // TILE, one, 0)

    def finish(way, shard, early):
        for chunk in range(CHUNKS - 1):
            compact(shard, chunk)

            def add(columns, chunk=chunk):
                value = product(routed_a[:, : widths[chunk]], starts[chunk], columns)
                total[:, columns] = value if chunk == 0 else total[:, columns] + value

            over_columns(add)

        @pl.when(jnp.logical_not(early))
        def _():
            take_routed(way, shard)

        def add_routed(columns):
            total[:, columns] = total[:, columns] + product(routed_b[shard], wide, columns)

        over_columns(add_routed)
        compact(shard, CHUNKS - 1)
        rows = pl.ds(pl.multiple_of(shard * group, 16), group)

        def write(columns):
            value = total[:, columns] + product(routed_a[:, : widths[-1]], starts[-1], columns)
            stage[0, rows, columns] = value.astype(jnp.bfloat16)

        over_columns(write)

    def take_to_pass(way, shard):
        @pl.when(has_next(way))
        def _():
            take_routed(way, shard)

    def along_routed(step, carry):
        on_line(step + 1, take_to_pass)

        def one(way, inner):
            shard = hid - step + 2 * step * way

            @pl.when((shard >= 0) & (shard < n_hid))
            def _():
                finish(way, shard, (step == 0) | has_next(way))

            return inner

        lax.fori_loop(0, jnp.where(step > 0, 2, 1), one, 0)
        return carry

    lax.fori_loop(0, n_hid, along_routed, 0)

    for shard in range(n_hid):
        for chunk in range(CHUNKS):
            sent_rows = send_a.at[shard, pl.ds(0, peers_rows), span(chunk)]
            pltpu.make_async_copy(sent_rows, sent_rows, a_send.at[shard, chunk]).wait()
        for way in range(2):
            sent = has_next(way) & ((shard <= hid) if way == 0 else (shard >= hid))

            @pl.when(sent)
            def _():
                for chunk in range(CHUNKS):
                    raw_copy(way, shard, chunk).wait_send()
                routed_copy(way, shard).wait_send()

    sent_rows = send_b.at[pl.ds(0, peers_rows)]
    pltpu.make_async_copy(sent_rows, sent_rows, b_send).wait()
    pltpu.make_async_copy(cnts.at[pl.ds(0, n_ex - 1)], cnts.at[pl.ds(0, n_ex - 1)], cnt_send).wait()
    for i in range(1, n_hid):
        meta_copy(i).wait_send()


def shards(n_ex, n_hid, cotangent, slot_token, slot_gate, w_down):
    tokens, features = cotangent.shape
    hidden = w_down.shape[1]
    slots = -(-slot_token.shape[2] // 16) * 16
    lanes = -(-2 * n_ex // 128) * 128
    wide = features * RAW_SHARE[0] // RAW_SHARE[1] // 128 * 128
    part = -(-wide // (TILE * CHUNKS)) * TILE
    widths = tuple(min(part, wide - chunk * part) for chunk in range(CHUNKS))
    narrow = features - wide
    group = CF * tokens
    dma = pltpu.SemaphoreType.DMA
    bf16, f32 = jnp.bfloat16, jnp.float32
    hbm = pl.BlockSpec(memory_space=pltpu.HBM)
    return pl.pallas_call(
        functools.partial(kernel, n_ex, n_hid, slots, widths),
        out_shape=pltpu.VMEM((1, n_hid * group, hidden), bf16),
        in_specs=[hbm, hbm, hbm, hbm],
        out_specs=pl.BlockSpec(memory_space=pltpu.VMEM),
        scratch_shapes=[
            pltpu.VMEM(cotangent.shape, bf16),
            pltpu.VMEM(slot_token.shape, jnp.int32),
            pltpu.VMEM(slot_gate.shape, f32),
            pltpu.VMEM((n_hid, n_ex * slots, tokens), bf16),
            pltpu.VMEM((n_hid, n_ex * slots, 128), f32),
            pltpu.VMEM((n_hid, group, n_ex * slots), bf16),
            pltpu.VMEM((features, hidden), bf16),
            pltpu.VMEM((group, hidden), f32),
            pltpu.VMEM((n_hid, tokens, wide), bf16),
            pltpu.VMEM((lanes, 128), f32),
            pltpu.VMEM((n_hid, slots, lanes), f32),
            pltpu.VMEM((-(-n_hid // 8) * 8, lanes), f32),
            pltpu.VMEM((n_ex, -(-n_hid // 8) * 8, lanes), f32),
            pltpu.VMEM((n_hid, n_ex * slots, wide), bf16),
            pltpu.VMEM((n_ex * slots, narrow), bf16),
            pltpu.VMEM((n_hid, n_ex * slots, wide), bf16),
            pltpu.VMEM((n_ex * slots, narrow), bf16),
            pltpu.VMEM((n_hid, group, narrow), bf16),
            pltpu.VMEM((group, part), bf16),
            pltpu.VMEM((2, TILE, features), bf16),
            dma((2, n_hid, CHUNKS)), dma((n_hid, CHUNKS)), dma((n_hid,)), dma((n_hid,)), dma, dma,
            dma((n_hid, CHUNKS)), dma((n_hid, CHUNKS)), dma, dma, dma((2, n_hid)), dma((n_hid,)), dma((5,)),
        ],
        compiler_params=pltpu.CompilerParams(
            collective_id=0, has_side_effects=True, vmem_limit_bytes=56 * 1024 * 1024
        ),
        cost_estimate=pl.CostEstimate(
            flops=2 * n_hid * group * hidden * features, bytes_accessed=2 * hidden * features * 3, transcendentals=0
        ),
        name="route_and_multiply",
    )(cotangent, slot_token, slot_gate, w_down)


def solution(mesh):
    n_ex, n_hid = mesh.shape["expert"], mesh.shape["hidden"]
    in_specs = (
        P(("expert", "hidden"), None),
        P(("expert", "hidden"), None, None),
        P(("expert", "hidden"), None, None),
        P("expert", "hidden", None),
    )
    out_specs = P("expert", None, "hidden")
    return jax.shard_map(
        functools.partial(shards, n_ex, n_hid), mesh=mesh, in_specs=in_specs, out_specs=out_specs, check_vma=False
    )
```

```python
import functools

import jax
import jax.numpy as jnp
from jax import lax
from jax.experimental import pallas as pl
from jax.experimental.pallas import tpu as pltpu
from jax.sharding import PartitionSpec as P

CF = 2
CHUNKS = 2
RAW_SHARE = 12, 16
TILE = 256
MESH = pl.DeviceIdType.MESH


def tile_of(width):
    return width if width <= 640 else TILE if width % TILE == 0 else 128


def kernel(
    n_ex, n_hid, slots, widths, cot_hbm, token_hbm, gate_hbm, w_hbm, stage,
    cot, token_in, gate_in, pick, gates, put, weight_t, total,
    raw, table, meta, cnt, cnts, send_a, send_b, got_a, got_b, routed_b, routed_a, weight,
    raw_send, raw_recv, meta_send, meta_recv, cnt_send, cnt_recv,
    a_send, a_recv, b_send, b_recv, rb_send, rb_recv, load_sem,
):
    ex, hid = lax.axis_index("expert"), lax.axis_index("hidden")
    tokens = cot.shape[0]
    def span(chunk):
        return pl.ds(starts[chunk], widths[chunk])

    starts = [sum(widths[:chunk]) for chunk in range(CHUNKS)]
    wide = sum(widths)
    narrow = send_b.shape[1]
    group = routed_b.shape[1]
    lanes = meta.shape[2]
    peers_rows = (n_ex - 1) * slots

    def rows_of(i):
        return pl.ds(pl.multiple_of(i * slots, 16), slots)

    loads = [
        pltpu.make_async_copy(source, target, load_sem.at[i])
        for i, (source, target) in enumerate(
            [(token_hbm, token_in), (gate_hbm, gate_in), (cot_hbm, cot)]
        )
    ]
    for load in loads:
        load.start()

    def weight_load(c):
        rows = pl.ds(c * TILE, TILE)
        return pltpu.make_async_copy(w_hbm.at[0, rows], weight.at[c % 2], load_sem.at[3 + c % 2])

    w_tiles = w_hbm.shape[1] // TILE
    for c in range(min(2, w_tiles)):
        weight_load(c).start()

    barrier = pltpu.get_barrier_semaphore()

    def greet_plane(i, carry):
        pl.semaphore_signal(barrier, inc=1, device_id={"expert": lax.rem(ex + i, n_ex)}, device_id_type=MESH)
        return carry

    def greet_line(i, carry):
        pl.semaphore_signal(barrier, inc=1, device_id={"hidden": lax.rem(hid + i, n_hid)}, device_id_type=MESH)
        return carry

    lax.fori_loop(1, n_ex, greet_plane, 0)
    lax.fori_loop(1, n_hid, greet_line, 0)

    def meta_copy(i):
        return pltpu.make_async_remote_copy(
            src_ref=meta.at[hid], dst_ref=meta.at[hid], send_sem=meta_send.at[i], recv_sem=meta_recv.at[hid],
            device_id={"hidden": lax.rem(hid + i, n_hid)}, device_id_type=MESH,
        )

    def to_next(src, dst, send, recv, way):
        return pltpu.make_async_remote_copy(
            src_ref=src, dst_ref=dst, send_sem=send, recv_sem=recv,
            device_id={"hidden": hid + 1 - 2 * way}, device_id_type=MESH,
        )

    def raw_copy(way, shard, chunk, own=False):
        held = raw.at[shard, :, span(chunk)]
        src = cot_hbm.at[:, pl.ds(starts[chunk], widths[chunk])] if own else held
        return to_next(src, held, raw_send.at[way, shard, chunk], raw_recv.at[shard, chunk], way)

    def routed_copy(way, shard):
        held = routed_b.at[shard]
        return to_next(held, held, rb_send.at[way, shard], rb_recv.at[shard], way)

    def has_next(way):
        after = hid + 1 - 2 * way
        return (after >= 0) & (after < n_hid)

    def both_ways(body):
        def step(way, carry):
            body(way)
            return carry

        lax.fori_loop(0, 2, step, 0)

    def start_raw(way, chunk):
        @pl.when(has_next(way))
        def _():
            raw_copy(way, hid, chunk, own=True).start()

    loads[0].wait()
    loads[1].wait()
    live_slots = token_in.shape[2]
    table[...] = jnp.where(lax.broadcasted_iota(jnp.int32, table.shape, 0) < n_ex, -1.0, 0.0)
    table[0:n_ex, 0:live_slots] = token_in[0].astype(jnp.float32)
    table[n_ex : 2 * n_ex, 0:live_slots] = gate_in[0]
    meta[hid] = table[...].T[0:slots, :]

    lane = lax.broadcasted_iota(jnp.int32, (slots, lanes), 1)
    token_iota = lax.broadcasted_iota(jnp.int32, (slots, tokens), 1).astype(jnp.float32)

    def choose(shard):
        held = meta[shard]

        def one(expert, carry):
            token = jnp.sum(jnp.where(lane == expert, held, 0.0), axis=1, keepdims=True)
            gate = jnp.sum(jnp.where(lane == expert + n_ex, held, 0.0), axis=1, keepdims=True)
            pick[shard, rows_of(expert), :] = jnp.where(token == token_iota, 1.0, 0.0).astype(jnp.bfloat16)
            gates[shard, rows_of(expert), :] = jnp.broadcast_to(gate, (slots, 128))
            return carry

        lax.fori_loop(0, n_ex, one, 0)

    def tile(c, base=0, size=TILE):
        return pl.ds(pl.multiple_of(base + c * size, 128), size)

    def scale(shard, rows, store, columns):
        size = tile_of(columns)

        def one(c, carry):
            rows_c = jnp.dot(pick[shard], rows(c, size), preferred_element_type=jnp.float32)
            gate = jnp.concatenate([gates[shard]] * (size // 128), axis=1)
            store(c, size, (gate * rows_c).astype(jnp.bfloat16))
            return carry

        lax.fori_loop(0, columns // size, one, 0)

    def a_copy(shard, chunk, expert):
        return pltpu.make_async_remote_copy(
            src_ref=send_a.at[shard, rows_of(expert), span(chunk)],
            dst_ref=got_a.at[shard, rows_of(ex), span(chunk)],
            send_sem=a_send.at[shard, chunk], recv_sem=a_recv.at[shard, chunk],
            device_id={"expert": expert}, device_id_type=MESH,
        )

    def b_copy(expert):
        return pltpu.make_async_remote_copy(
            src_ref=send_b.at[rows_of(expert)], dst_ref=got_b.at[rows_of(ex)],
            send_sem=b_send, recv_sem=b_recv, device_id={"expert": expert}, device_id_type=MESH,
        )

    def store_narrow(c, size, value):
        send_b[:, tile(c, 0, size)] = value

    def start_narrow(i, carry):
        b_copy(lax.rem(ex + i, n_ex)).start()
        return carry

    choose(hid)
    pl.semaphore_wait(barrier, n_ex + n_hid - 2)
    for chunk in range(CHUNKS):
        both_ways(functools.partial(start_raw, chunk=chunk))
    for i in range(1, n_hid):
        meta_copy(i).start()
    loads[2].wait()
    scale(hid, lambda c, size: cot[:, tile(c, wide, size)], store_narrow, narrow)
    lax.fori_loop(1, n_ex, start_narrow, 0)
    got_b[rows_of(ex), :] = send_b[rows_of(ex), :]

    def send_wide(shard, chunk, rows):
        def store_wide(c, size, value):
            send_a[shard, :, tile(c, starts[chunk], size)] = value

        def start_wide(i, carry):
            a_copy(shard, chunk, lax.rem(ex + i, n_ex)).start()
            return carry

        scale(shard, rows, store_wide, widths[chunk])
        lax.fori_loop(1, n_ex, start_wide, 0)
        got_a[shard, rows_of(ex), span(chunk)] = send_a[shard, rows_of(ex), span(chunk)]

    for chunk in range(CHUNKS):
        send_wide(hid, chunk, lambda c, size: cot[:, tile(c, starts[chunk], size)])

    for i in range(1, n_hid):
        source = lax.rem(hid + i, n_hid)
        pltpu.make_async_copy(meta.at[source], meta.at[source], meta_recv.at[source]).wait()
    cnt[...] = jnp.zeros(cnt.shape, cnt.dtype)
    for shard in range(n_hid):
        live = jnp.where((meta[shard] >= 0.0) & (lane < n_ex), 1.0, 0.0)
        cnt[shard : shard + 1, :] = jnp.sum(live, axis=0, keepdims=True)

    def cnt_copy(i):
        return pltpu.make_async_remote_copy(
            src_ref=cnt, dst_ref=cnts.at[ex], send_sem=cnt_send, recv_sem=cnt_recv,
            device_id={"expert": lax.rem(ex + i, n_ex)}, device_id_type=MESH,
        )

    def send_cnt(i, carry):
        cnt_copy(i).start()
        return carry

    lax.fori_loop(1, n_ex, send_cnt, 0)
    cnts[ex] = cnt[...]
    pltpu.make_async_copy(cnts.at[pl.ds(0, n_ex - 1)], cnts.at[pl.ds(0, n_ex - 1)], cnt_recv).wait()

    one_lane = lax.broadcasted_iota(jnp.int32, (1, lanes), 1)

    def order(shard):
        number = lax.broadcasted_iota(jnp.int32, (1, n_ex * slots), 1).astype(jnp.float32)
        owner = jnp.floor((number + 0.5) / slots)
        place = number - owner * slots

        def add(source, carry):
            first, own = carry
            row = cnts[source, pl.ds(shard, 1), :]
            count = jnp.sum(jnp.where(one_lane == ex, row, 0.0), axis=1, keepdims=True)
            at = source.astype(jnp.float32)
            return first + jnp.where(owner > at, count, 0.0), own + jnp.where(owner == at, count, 0.0)

        zero = jnp.zeros(owner.shape, jnp.float32)
        first, own = lax.fori_loop(0, n_ex, add, (zero, zero))
        target = jnp.where(place < own, first + place, -1.0)
        row = lax.broadcasted_iota(jnp.int32, (group, owner.shape[1]), 0).astype(jnp.float32)
        put[shard] = jnp.where(row == target, 1.0, 0.0).astype(jnp.bfloat16)

    order(hid)

    pltpu.make_async_copy(got_b.at[pl.ds(0, peers_rows)], got_b.at[pl.ds(0, peers_rows)], b_recv).wait()
    routed_b[hid] = jnp.dot(put[hid], got_b[...], preferred_element_type=jnp.float32).astype(jnp.bfloat16)

    def start_routed(way):
        @pl.when(has_next(way))
        def _():
            routed_copy(way, hid).start()

    def on_line(step, body):
        def one(way):
            shard = hid - step + 2 * step * way

            @pl.when((shard >= 0) & (shard < n_hid))
            def _():
                body(way, shard)

        both_ways(one)

    def take_raw(way, shard, chunk):
        held = raw.at[shard, :, span(chunk)]
        pltpu.make_async_copy(held, held, raw_recv.at[shard, chunk]).wait()

        @pl.when(has_next(way))
        def _():
            raw_copy(way, shard, chunk).start()

        send_wide(shard, chunk, lambda c, size: raw[shard, :, tile(c, starts[chunk], size)])

    def take_routed(way, shard):
        pltpu.make_async_copy(routed_b.at[shard], routed_b.at[shard], rb_recv.at[shard]).wait()

        @pl.when(has_next(way))
        def _():
            routed_copy(way, shard).start()

    def along(step, carry):
        for chunk in range(CHUNKS):
            on_line(step, functools.partial(take_raw, chunk=chunk))
        last_raw(step)
        return carry

    def last_raw(step):
        def one(way):
            @pl.when(step == hid + way * (n_hid - 1 - 2 * hid))
            def _():
                start_routed(way)

        both_ways(one)

    last_raw(0)

    def order_other(i, carry):
        shard = lax.rem(hid + i, n_hid)
        choose(shard)
        order(shard)
        return carry

    lax.fori_loop(1, n_hid, order_other, 0)
    for c in range(w_tiles):
        weight_load(c).wait()
        weight_t[:, c * TILE : (c + 1) * TILE] = weight[c % 2].T
        if c + 2 < w_tiles:
            weight_load(c + 2).start()

    lax.fori_loop(1, n_hid, along, 0)

    def product(lhs, row, columns):
        return jnp.dot(lhs, weight_t[row : row + lhs.shape[1], columns], preferred_element_type=jnp.float32)

    def compact(shard, chunk):
        if n_ex > 1:
            arrived = got_a.at[shard, pl.ds(0, peers_rows), span(chunk)]
            pltpu.make_async_copy(arrived, arrived, a_recv.at[shard, chunk]).wait()

        def one(c, carry):
            columns = tile(c, 0, size)
            rows = jnp.dot(put[shard], got_a[shard, :, tile(c, starts[chunk], size)], preferred_element_type=jnp.float32)
            routed_a[:, columns] = rows.astype(jnp.bfloat16)
            return carry

        size = tile_of(widths[chunk])
        lax.fori_loop(0, widths[chunk] // size, one, 0)

    def over_columns(body):
        def one(c, carry):
            body(tile(c))
            return carry

        lax.fori_loop(0, stage.shape[2] // TILE, one, 0)

    def finish(way, shard, early):
        for chunk in range(CHUNKS - 1):
            compact(shard, chunk)

            def add(columns, chunk=chunk):
                value = product(routed_a[:, : widths[chunk]], starts[chunk], columns)
                total[:, columns] = value if chunk == 0 else total[:, columns] + value

            over_columns(add)

        @pl.when(jnp.logical_not(early))
        def _():
            take_routed(way, shard)

        def add_routed(columns):
            total[:, columns] = total[:, columns] + product(routed_b[shard], wide, columns)

        over_columns(add_routed)
        compact(shard, CHUNKS - 1)
        rows = pl.ds(pl.multiple_of(shard * group, 16), group)

        def write(columns):
            value = total[:, columns] + product(routed_a[:, : widths[-1]], starts[-1], columns)
            stage[0, rows, columns] = value.astype(jnp.bfloat16)

        over_columns(write)

    def take_to_pass(way, shard):
        @pl.when(has_next(way))
        def _():
            take_routed(way, shard)

    def along_routed(step, carry):
        on_line(step + 1, take_to_pass)

        def one(way, inner):
            shard = hid - step + 2 * step * way

            @pl.when((shard >= 0) & (shard < n_hid))
            def _():
                finish(way, shard, (step == 0) | has_next(way))

            return inner

        lax.fori_loop(0, jnp.where(step > 0, 2, 1), one, 0)
        return carry

    lax.fori_loop(0, n_hid, along_routed, 0)

    for shard in range(n_hid):
        for chunk in range(CHUNKS):
            sent_rows = send_a.at[shard, pl.ds(0, peers_rows), span(chunk)]
            pltpu.make_async_copy(sent_rows, sent_rows, a_send.at[shard, chunk]).wait()
        for way in range(2):
            sent = has_next(way) & ((shard <= hid) if way == 0 else (shard >= hid))

            @pl.when(sent)
            def _():
                for chunk in range(CHUNKS):
                    raw_copy(way, shard, chunk).wait_send()
                routed_copy(way, shard).wait_send()

    sent_rows = send_b.at[pl.ds(0, peers_rows)]
    pltpu.make_async_copy(sent_rows, sent_rows, b_send).wait()
    pltpu.make_async_copy(cnts.at[pl.ds(0, n_ex - 1)], cnts.at[pl.ds(0, n_ex - 1)], cnt_send).wait()
    for i in range(1, n_hid):
        meta_copy(i).wait_send()


def shards(n_ex, n_hid, cotangent, slot_token, slot_gate, w_down):
    tokens, features = cotangent.shape
    hidden = w_down.shape[1]
    slots = -(-slot_token.shape[2] // 16) * 16
    lanes = -(-2 * n_ex // 128) * 128
    wide = features * RAW_SHARE[0] // RAW_SHARE[1] // 128 * 128
    part = -(-wide // (TILE * CHUNKS)) * TILE
    widths = tuple(min(part, wide - chunk * part) for chunk in range(CHUNKS))
    narrow = features - wide
    group = CF * tokens
    dma = pltpu.SemaphoreType.DMA
    bf16, f32 = jnp.bfloat16, jnp.float32
    hbm = pl.BlockSpec(memory_space=pltpu.HBM)
    return pl.pallas_call(
        functools.partial(kernel, n_ex, n_hid, slots, widths),
        out_shape=pltpu.VMEM((1, n_hid * group, hidden), bf16),
        in_specs=[hbm, hbm, hbm, hbm],
        out_specs=pl.BlockSpec(memory_space=pltpu.VMEM),
        scratch_shapes=[
            pltpu.VMEM(cotangent.shape, bf16),
            pltpu.VMEM(slot_token.shape, jnp.int32),
            pltpu.VMEM(slot_gate.shape, f32),
            pltpu.VMEM((n_hid, n_ex * slots, tokens), bf16),
            pltpu.VMEM((n_hid, n_ex * slots, 128), f32),
            pltpu.VMEM((n_hid, group, n_ex * slots), bf16),
            pltpu.VMEM((features, hidden), bf16),
            pltpu.VMEM((group, hidden), f32),
            pltpu.VMEM((n_hid, tokens, wide), bf16),
            pltpu.VMEM((lanes, 128), f32),
            pltpu.VMEM((n_hid, slots, lanes), f32),
            pltpu.VMEM((-(-n_hid // 8) * 8, lanes), f32),
            pltpu.VMEM((n_ex, -(-n_hid // 8) * 8, lanes), f32),
            pltpu.VMEM((n_hid, n_ex * slots, wide), bf16),
            pltpu.VMEM((n_ex * slots, narrow), bf16),
            pltpu.VMEM((n_hid, n_ex * slots, wide), bf16),
            pltpu.VMEM((n_ex * slots, narrow), bf16),
            pltpu.VMEM((n_hid, group, narrow), bf16),
            pltpu.VMEM((group, part), bf16),
            pltpu.VMEM((2, TILE, features), bf16),
            dma((2, n_hid, CHUNKS)), dma((n_hid, CHUNKS)), dma((n_hid,)), dma((n_hid,)), dma, dma,
            dma((n_hid, CHUNKS)), dma((n_hid, CHUNKS)), dma, dma, dma((2, n_hid)), dma((n_hid,)), dma((5,)),
        ],
        compiler_params=pltpu.CompilerParams(
            collective_id=0, has_side_effects=True, vmem_limit_bytes=56 * 1024 * 1024
        ),
        cost_estimate=pl.CostEstimate(
            flops=2 * n_hid * group * hidden * features, bytes_accessed=2 * hidden * features * 3, transcendentals=0
        ),
        name="route_and_multiply",
    )(cotangent, slot_token, slot_gate, w_down)


def solution(mesh):
    n_ex, n_hid = mesh.shape["expert"], mesh.shape["hidden"]
    in_specs = (
        P(("expert", "hidden"), None),
        P(("expert", "hidden"), None, None),
        P(("expert", "hidden"), None, None),
        P("expert", "hidden", None),
    )
    out_specs = P("expert", None, "hidden")
    return jax.shard_map(
        functools.partial(shards, n_ex, n_hid), mesh=mesh, in_specs=in_specs, out_specs=out_specs, check_vma=False
    )
```
